32 devices in a mesh: parts: 2 (over y), tensor: 4 (over z), fsdp: 4 (over x, core).
Axes of the slice: x: 2, y: 2, z: 4, core: 2. Of those that a mesh axis runs over, the one named last changes fastest.
Arguments:
- tokens: bfloat16 [1024, 4096], P(('parts', 'fsdp'), 'tensor'), parts along dimension 0, may hold values from -6 to 6
- cotangent: bfloat16 [1024, 4096], P(('parts', 'fsdp'), 'tensor'), parts along dimension 0, may hold values from -6 to 6
- gate_values: bfloat16 [8, 160, 128, 128], P('fsdp', 'tensor'), may hold values from -0.1875 to 0.1875
- gate_rows: int32 [8, 160], P('fsdp', 'tensor'), may hold values from 0 to 31, as said below
- gate_scale: bfloat16 [8, 160], P('fsdp', 'tensor'), may hold values from 0.5 to 2
- up_values: bfloat16 [8, 160, 128, 128], P('fsdp', 'tensor'), may hold values from -0.1875 to 0.1875
- up_rows: int32 [8, 160], P('fsdp', 'tensor'), may hold values from 0 to 31, as said below
- up_scale: bfloat16 [8, 160], P('fsdp', 'tensor'), may hold values from 0.5 to 2
- down_values: bfloat16 [8, 160, 128, 128], P('fsdp', 'tensor'), may hold values from -0.078125 to 0.078125
- down_cols: int32 [8, 160], P('fsdp', 'tensor'), may hold values from 0 to 31, as said below
- down_scale: bfloat16 [8, 160], P('fsdp', 'tensor'), may hold values from 0.5 to 2
Outputs:
- layer_out: bfloat16 [1024, 4096], P(('parts', 'fsdp'), 'tensor'), parts along dimension 0
- grad_tokens: bfloat16 [1024, 4096], P(('parts', 'fsdp'), 'tensor'), parts along dimension 0
- grad_gate: bfloat16 [16, 160, 128, 128], P(('parts', 'fsdp'), 'tensor'), parts along dimension 0
- grad_up: bfloat16 [16, 160, 128, 128], P(('parts', 'fsdp'), 'tensor'), parts along dimension 0
- grad_down: bfloat16 [16, 160, 128, 128], P(('parts', 'fsdp'), 'tensor'), parts along dimension 0
The draws below stay inside these ranges and needn't reach their ends.
There are 2 independent parts, one for each index of `parts`. The reference program is written for one: setup_inputs(seed, part) draws one part's arguments, and reference() takes and returns one part's arrays. A program takes and returns all parts, laid end to end along the dimension named above; an argument that names none is the same for every part. Nothing has to cross between parts.
Inputs may be any that keep to these rules, and one draw needn't show every extreme that they name: `gate_rows`: the 8 entries of each column name distinct input blocks; some input blocks are named far more often than others. `up_rows`: the 8 entries of each column name distinct input blocks; some input blocks are named far more often than others. `down_cols`: the 8 entries of each column name distinct output blocks; some output blocks are named far more often than others.
All inputs are finite; a program needn't handle non-finite values.
Results may differ from the reference program's by a relative error of at most 0.023.
Values may be sent and summed in bfloat16 or wider, within the bound.
No kernel may reach another device: no remote copies, remote signals or barrier semaphores. Data moves between devices by JAX's collectives and lax.ppermute only.
A program may use at most 192 MiB of HBM per device.

```python
import math
import jax
import jax.numpy as jnp
from jax import lax

D = 4096
FF = 20480
BLK = 128
K = 8
TOK_DEV = 128
TOKENS = 512
N_FSDP = 4


def pick_blocks(key):
    nblocks = D // BLK
    ncolumns = FF // BLK
    popular = jax.random.randint(jax.random.fold_in(key, 1), (nblocks,), 0, 1 << 20)
    noise = jax.random.randint(jax.random.fold_in(key, 2), (ncolumns, nblocks), 0, 1 << 20)
    column_ids = jnp.arange(ncolumns, dtype=jnp.int32)[:, None]
    block_ids = jnp.arange(nblocks, dtype=jnp.int32)[None, :]
    forced = (column_ids == 0) & (block_ids == 0) | (column_ids == 1) & (block_ids == nblocks - 1)
    scores = (noise + popular[None, :] + forced.astype(jnp.int32) * (1 << 22)) * nblocks + block_ids
    chosen = lax.top_k(scores, K)[1]
    return jnp.transpose(chosen).astype(jnp.int32)


def draw_gate_rows(key, part):
    return pick_blocks(jax.random.fold_in(key, 11))


def draw_up_rows(key, part):
    return pick_blocks(jax.random.fold_in(key, 12))


def draw_down_cols(key, part):
    return pick_blocks(jax.random.fold_in(key, 13))


def block_levels(own_key, shape, shards, smallest, largest):
    gain = 1.0
    for dim, shards_of in shards:
        steps = jax.random.uniform(jax.random.fold_in(jax.random.fold_in(own_key, 6), dim), (shards_of,), jnp.float32, smallest / len(shards), largest / len(shards))
        gain = gain * jnp.repeat(jnp.exp(steps), shape[dim] // shards_of).reshape((-1,) + (1,) * (len(shape) - 1 - dim))
    return gain


def normal_values(rng, dims, scale, limit, shards=(), kind=jnp.bfloat16):
    values = jax.random.normal(rng, dims, jnp.float32) * scale
    if len(shards) > 0:
        values = block_levels(rng, dims, shards, -0.22, 0.18) * values
    return jnp.clip(values, min=-limit, max=limit).astype(kind)


def setup_inputs(seed: int = 0, part: int = 0) -> dict:
    seeds = jax.random.split(jax.random.key(seed), 12)
    part_splits = jax.random.split(jax.random.fold_in(seeds[11], part), 12)
    tokens = normal_values(part_splits[0], (TOKENS, D), 1.0, 6.0, ((0, 4), (1, 4)))
    cotangent = normal_values(part_splits[1], (TOKENS, D), 0.5, 6.0, ((0, 4), (1, 4)))
    gate_values = normal_values(seeds[2], (K, FF // BLK, BLK, BLK), (K * BLK) ** -0.5, 0.1875, ((0, 4), (1, 4)))
    gate_rows = draw_gate_rows(jax.random.fold_in(seeds[11], 71), part)
    gate_scale = jnp.clip(jnp.exp(math.log(2.0) - 1.3862944 * jax.random.uniform(seeds[4], (K, FF // BLK), jnp.float32) ** block_levels(seeds[4], (K, FF // BLK), ((0, 4), (1, 4)), -0.2, 0.2)), 0.5, 2.0).astype(jnp.bfloat16)
    up_values = normal_values(seeds[5], (K, FF // BLK, BLK, BLK), (K * BLK) ** -0.5, 0.1875, ((0, 4), (1, 4)))
    up_rows = draw_up_rows(jax.random.fold_in(seeds[11], 71), part)
    up_scale = jnp.clip(jnp.exp(math.log(2.0) - 1.3862944 * jax.random.uniform(seeds[7], (K, FF // BLK), jnp.float32) ** block_levels(seeds[7], (K, FF // BLK), ((0, 4), (1, 4)), -0.2, 0.2)), 0.5, 2.0).astype(jnp.bfloat16)
    down_values = normal_values(seeds[8], (K, FF // BLK, BLK, BLK), (FF * K // (D // BLK)) ** -0.5, 0.078125, ((0, 4), (1, 4)))
    down_cols = draw_down_cols(jax.random.fold_in(seeds[11], 71), part)
    down_scale = jnp.clip(jnp.exp(math.log(2.0) - 1.3862944 * jax.random.uniform(seeds[10], (K, FF // BLK), jnp.float32) ** block_levels(seeds[10], (K, FF // BLK), ((0, 4), (1, 4)), -0.2, 0.2)), 0.5, 2.0).astype(jnp.bfloat16)
    return dict(tokens=tokens, cotangent=cotangent, gate_values=gate_values, gate_rows=gate_rows, gate_scale=gate_scale, up_values=up_values, up_rows=up_rows, up_scale=up_scale, down_values=down_values, down_cols=down_cols, down_scale=down_scale)


def weighted(selected, blocks, factors):
    products = jnp.einsum('tka,kab->tkb', selected, blocks.astype(jnp.float32))
    return jnp.sum(products * factors.astype(jnp.float32)[None, :, None], axis=1)


def rounded(values):
    return lax.optimization_barrier(values.astype(jnp.bfloat16)).astype(jnp.float32)


def group_sum(left, right, form, factors):
    left_groups = left.reshape((N_FSDP, TOK_DEV) + left.shape[1:])
    right_groups = right.reshape((N_FSDP, TOK_DEV) + right.shape[1:])
    terms = jnp.einsum(form, left_groups, right_groups) * factors.astype(jnp.float32)[None, :, None, None]
    return jnp.sum(rounded(terms), axis=0)


def reference(tokens, cotangent, gate_values, gate_rows, gate_scale, up_values, up_rows, up_scale, down_values, down_cols, down_scale):
    nblocks = D // BLK
    token_total = TOKENS
    x_blocks = tokens.reshape(token_total, nblocks, BLK).astype(jnp.float32)
    grad_blocks = cotangent.reshape(token_total, nblocks, BLK).astype(jnp.float32)
    columns = tuple(jnp.swapaxes(item, 0, 1) for item in (gate_values, gate_rows, gate_scale, up_values, up_rows, up_scale, down_values, down_cols, down_scale))

    def forward(out_sum, column):
        gate_blocks, gate_where, gate_factor, up_blocks, up_where, up_factor, down_blocks, down_where, down_factor = column
        gate_pre = weighted(x_blocks[:, gate_where], gate_blocks, gate_factor)
        up_pre = weighted(x_blocks[:, up_where], up_blocks, up_factor)
        hidden = rounded(gate_pre * jax.nn.sigmoid(gate_pre) * up_pre)
        pieces = jnp.einsum('tb,kbc->tkc', hidden, down_blocks.astype(jnp.float32)) * down_factor.astype(jnp.float32)[None, :, None]
        out_sum = out_sum.at[:, down_where].add(pieces)
        return out_sum, (gate_pre, up_pre, hidden)

    empty_sum = jnp.zeros((token_total, nblocks, BLK), jnp.float32)
    out_sum, saved = lax.scan(forward, empty_sum, columns)
    layer_out = out_sum.reshape(token_total, D).astype(jnp.bfloat16)

    def backward(in_sum, inputs):
        column, kept = inputs
        gate_blocks, gate_where, gate_factor, up_blocks, up_where, up_factor, down_blocks, down_where, down_factor = column
        gate_pre, up_pre, hidden = kept
        down_sel = grad_blocks[:, down_where]
        grad_hidden = jnp.sum(jnp.einsum('tkc,kbc->tkb', down_sel, down_blocks.astype(jnp.float32)) * down_factor.astype(jnp.float32)[None, :, None], axis=1)
        sigmoid_gate = jax.nn.sigmoid(gate_pre)
        grad_gate_act = rounded(grad_hidden * up_pre * sigmoid_gate * (1.0 + gate_pre * (1.0 - sigmoid_gate)))
        grad_up_act = rounded(grad_hidden * gate_pre * sigmoid_gate)
        gate_sel = x_blocks[:, gate_where]
        up_sel = x_blocks[:, up_where]
        down_part = group_sum(hidden, down_sel, 'qtb,qtkc->qkbc', down_factor)
        gate_part = group_sum(gate_sel, grad_gate_act, 'qtka,qtb->qkab', gate_factor)
        up_part = group_sum(up_sel, grad_up_act, 'qtka,qtb->qkab', up_factor)
        back_gate = jnp.einsum('tb,kab->tka', grad_gate_act, gate_blocks.astype(jnp.float32)) * gate_factor.astype(jnp.float32)[None, :, None]
        back_up = jnp.einsum('tb,kab->tka', grad_up_act, up_blocks.astype(jnp.float32)) * up_factor.astype(jnp.float32)[None, :, None]
        in_sum = in_sum.at[:, gate_where].add(back_gate)
        in_sum = in_sum.at[:, up_where].add(back_up)
        return in_sum, (gate_part, up_part, down_part)

    in_sum, grads = lax.scan(backward, empty_sum, (columns, saved))
    grad_tokens = in_sum.reshape(token_total, D).astype(jnp.bfloat16)
    grad_gate = jnp.swapaxes(grads[0], 0, 1).astype(jnp.bfloat16)
    grad_up = jnp.swapaxes(grads[1], 0, 1).astype(jnp.bfloat16)
    grad_down = jnp.swapaxes(grads[2], 0, 1).astype(jnp.bfloat16)
    return (layer_out, grad_tokens, grad_gate, grad_up, grad_down)
```

```python
import functools

import jax
import jax.numpy as jnp
from jax import lax
from jax.experimental import pallas as pl
from jax.experimental.pallas import tpu as pltpu
from jax.sharding import PartitionSpec as P

F32, BF16 = jnp.float32, jnp.bfloat16


def dot(a, b, ca, cb):
    return lax.dot_general(a, b, (((ca,), (cb,)), ((), ())), preferred_element_type=F32)


def column_kernel(first, last, sizes, own_slots, slots, *refs):
    refs = list(refs)
    take = lambda n: [refs.pop(0) for _ in range(n)]
    cols, half_cols, rows, scales, me = take(5)
    own = take(3)
    (mate,) = take(1)
    other = take(len(sizes))
    x_own, x_mate, xt_own, xt_mate = take(4)
    g_parts = take(4)
    sums_in = None
    if not first:
        (sums_in,) = take(1)
        take(4)
    grads = take(3)
    (grad_mate,) = take(1)
    if last:
        out_keep, out_send = take(2)
    else:
        (sums_out,) = take(1)
    x_s, xt_s, g_s, acc, ws, stage, sems = refs
    i = pl.program_id(0)
    n = pl.num_programs(0)
    core = me[0]
    nblocks, tokens, block = x_s.shape
    quarter = tokens // 4
    groups = x_own.shape[0]
    run = x_own.shape[1]

    def copies_x():
        out = []
        for z in range(groups):
            for where, src, srct in ((core, x_own, xt_own), (1 - core, x_mate, xt_mate)):
                at = pl.ds(z * 2 * run + where * run, run)
                out.append(pltpu.make_async_copy(src.at[z], x_s.at[at], sems.at[0]))
        return out

    def copies_xt():
        out = []
        for z in range(groups):
            for where, src, srct in ((core, x_own, xt_own), (1 - core, x_mate, xt_mate)):
                at = pl.ds(z * 2 * run + where * run, run)
                out.append(pltpu.make_async_copy(srct.at[z], xt_s.at[at], sems.at[1]))
        return out

    def copies_g():
        out = []
        for j, part in enumerate(g_parts):
            where = core if j % 2 == 0 else 1 - core
            at = pl.ds(pl.multiple_of((j // 2) * 2 * quarter + where * quarter, quarter), quarter)
            out.append(pltpu.make_async_copy(part, g_s.at[:, at, :], sems.at[2]))
        return out

    def copies_sums():
        return [pltpu.make_async_copy(sums_in, acc, sems.at[3])]

    @pl.when(i == 0)
    def _():
        for c in copies_x() + copies_g() + copies_xt():
            c.start()
        if not first:
            for c in copies_sums():
                c.start()
        for c in copies_x():
            c.wait()

    base = half_cols[i] * 3 * slots

    def row(m, k):
        return rows[base + m * slots + k]

    def scale(m, k):
        return scales[base + m * slots + k]

    half = slots // 2
    for m in range(3):
        for k in range(own_slots):
            ws[m, k] = own[m][k, 0] * scale(m, k).astype(BF16)
            ws[m, own_slots + k] = mate[m, k, 0] * scale(m, own_slots + k).astype(BF16)
    start = 0
    for ref, size in zip(other, sizes):

        def fill(ref=ref):
            for m in range(3):
                for k in range(half):
                    ws[m, half + k] = ref[m, k, 0] * scale(m, half + k).astype(BF16)

        if len(sizes) == 1:
            fill()
        else:
            pl.when((i >= start) & (i < start + size))(fill)
        start += size

    def select(src, m, count):
        return jnp.concatenate([src[row(m, k)] for k in range(count)], axis=1)

    gate_w = ws[0].reshape(slots * block, block)
    up_w = ws[1].reshape(slots * block, block)
    gate_pre = dot(select(x_s, 0, slots), gate_w, 1, 0)
    up_pre = dot(select(x_s, 1, slots), up_w, 1, 0)

    @pl.when(i == 0)
    def _():
        for c in copies_g():
            c.wait()

    down_w = jnp.concatenate([ws[2, k] for k in range(slots)], axis=1)
    grad_hidden = dot(select(g_s, 2, slots), down_w, 1, 1)
    s = jax.nn.sigmoid(gate_pre)
    activated = gate_pre * s
    hidden = (activated * up_pre).astype(BF16)
    gate_act = (grad_hidden * up_pre * s * (1.0 + gate_pre * (1.0 - s))).astype(BF16)
    up_act = (grad_hidden * activated).astype(BF16)

    @pl.when(i == 0)
    def _():
        for c in copies_xt():
            c.wait()
        if first:
            acc[...] = jnp.zeros(acc.shape, F32)
        else:
            for c in copies_sums():
                c.wait()

    for m, act in ((0, gate_act), (1, up_act)):
        lhs = jnp.concatenate([xt_s[row(m, k)] for k in range(half)], axis=0)
        g = dot(lhs, act, 1, 0)
        for k in range(half):
            piece = (g[k * block : (k + 1) * block] * scale(m, k)).astype(BF16)
            if k < own_slots:
                grads[m][k, 0] = piece
            else:
                grad_mate[m, k - own_slots, 0] = piece
    g = dot(hidden, select(g_s, 2, half), 0, 0)
    for k in range(half):
        piece = (g[:, k * block : (k + 1) * block] * scale(2, k)).astype(BF16)
        if k < own_slots:
            grads[2][k, 0] = piece
        else:
            grad_mate[2, k - own_slots, 0] = piece

    mine = tokens // 2
    out = dot(hidden[:mine], down_w, 1, 0)
    for k in range(slots):
        acc[0, row(2, k)] += out[:, k * block : (k + 1) * block]
    back = dot(gate_act[:mine], gate_w, 1, 1)
    for k in range(slots):
        acc[1, row(0, k)] += back[:, k * block : (k + 1) * block]
    back = dot(up_act[:mine], up_w, 1, 1)
    for k in range(slots):
        acc[1, row(1, k)] += back[:, k * block : (k + 1) * block]

    @pl.when(i == n - 1)
    def _():
        if last:
            keep = pl.ds(pl.multiple_of(core * quarter, quarter), quarter)
            send = pl.ds(pl.multiple_of((1 - core) * quarter, quarter), quarter)
            moves = []
            for a in range(2):
                for j, (at, dst) in enumerate(((keep, out_keep), (send, out_send))):
                    stage[a, j] = acc[a, :, at, :].astype(BF16)
                    for z in range(groups):
                        piece = stage.at[a, j, pl.ds(z * 2 * run, 2 * run)]
                        moves.append(pltpu.make_async_copy(piece, dst.at[z, a], sems.at[4]))
                        moves[-1].start()
            for c in moves:
                c.wait()
        else:
            c = pltpu.make_async_copy(acc, sums_out, sems.at[4])
            c.start()
            c.wait()


def columns_call(first, last, sizes, cols, half_cols, rows, scales, me, own, mate, other,
                 x_parts, xt_parts, g_parts, carried):
    own_slots, all_cols, block, _ = own[0].shape
    slots = 4 * own_slots
    n = sum(sizes)
    tokens = x_parts[0].shape[2]
    nblocks = g_parts[0].shape[0]
    any_spec = pl.BlockSpec(memory_space=pl.ANY)
    own_spec = pl.BlockSpec((own_slots, 1, block, block), lambda i, c, h, *_: (0, c[i], 0, 0))
    mate_spec = pl.BlockSpec((3, own_slots, 1, block, block), lambda i, c, h, *_: (0, 0, h[i], 0, 0))
    other_specs, start = [], 0
    for size in sizes:
        other_specs.append(pl.BlockSpec(
            (3, 2 * own_slots, 1, block, block),
            lambda i, *_, start=start, size=size: (0, 0, jnp.clip(i - start, 0, size - 1), 0, 0)))
        start += size
    in_specs = [own_spec] * 3 + [mate_spec] + other_specs + [any_spec] * 8
    args = [*own, mate, *other, *x_parts, *xt_parts, *g_parts]
    aliases = {}
    half_count = mate.shape[2]
    out_shape = [jax.ShapeDtypeStruct(own[0].shape, BF16)] * 3 + [jax.ShapeDtypeStruct((3, own_slots, half_count, block, block), BF16)]
    out_specs = [own_spec] * 3 + [mate_spec]
    if not first:
        at = 5 + len(args)
        args += list(carried)
        in_specs += [any_spec] * 5
        aliases = {at + 1 + j: j for j in range(4)}
        if not last:
            aliases[at] = 4
    if last:
        groups = x_parts[0].shape[0]
        out_shape += [jax.ShapeDtypeStruct((groups, 2, nblocks // groups, tokens // 4, block), BF16)] * 2
        out_specs += [any_spec] * 2
    else:
        out_shape += [jax.ShapeDtypeStruct((2, nblocks, tokens // 2, block), F32)]
        out_specs += [any_spec]
    stage_shape = (2, 2, nblocks, tokens // 4, block) if last else (1, 1, 8, 16, block)
    return pl.pallas_call(
        functools.partial(column_kernel, first, last, sizes, own_slots, slots),
        grid_spec=pltpu.PrefetchScalarGridSpec(
            num_scalar_prefetch=5, grid=(n,), in_specs=in_specs, out_specs=out_specs,
            scratch_shapes=[
                pltpu.VMEM((nblocks, tokens, block), BF16),
                pltpu.VMEM((nblocks, block, tokens), BF16),
                pltpu.VMEM((nblocks, tokens, block), BF16),
                pltpu.VMEM((2, nblocks, tokens // 2, block), F32),
                pltpu.VMEM((3, slots, block, block), BF16),
                pltpu.VMEM(stage_shape, BF16),
                pltpu.SemaphoreType.DMA((5,)),
            ]),
        out_shape=out_shape,
        input_output_aliases=aliases,
        compiler_params=pltpu.CompilerParams(vmem_limit_bytes=52 * 2**20),
        name="columns",
    )(cols, half_cols, rows, scales, me, *args)


CHUNKS = (4, 3, 2, 1)
CALLS = (("a0",), ("b0", "a1"), ("b1", "a2"), ("b2", "a3", "b3"))


def to_blocks(v, block):
    return jnp.swapaxes(v.reshape(v.shape[0], -1, block), 0, 1)


def local_pairs(tokens, cotangent, gate_values, gate_rows, gate_scale, up_values, up_rows, up_scale,
                down_values, down_cols, down_scale):
    own = (gate_values, up_values, down_values)
    own_slots, columns, block, _ = gate_values.shape
    half = columns // 2
    per_part = half // 2
    f = lax.axis_index("fsdp")
    core = lax.rem(f, 2)
    part = lax.axis_index("parts")
    swap_core = lambda v: lax.ppermute(v, "fsdp", [(i, i ^ 1) for i in range(4)])
    swap_chip = lambda v: lax.ppermute(v, "fsdp", [(i, i ^ 2) for i in range(4)])
    swap_part = lambda v: lax.ppermute(v, "parts", [(0, 1), (1, 0)])

    packed = jnp.stack([v.astype(F32) for v in (gate_rows, up_rows, down_cols, gate_scale, up_scale, down_scale)])
    packed = lax.all_gather(packed, "fsdp")
    packed = jnp.take(packed, f ^ jnp.arange(4), axis=0)
    packed = lax.dynamic_slice_in_dim(packed, core * half, half, axis=3)
    packed = jnp.transpose(packed, (1, 3, 0, 2)).reshape(2, 3, half, -1)
    packed = jnp.swapaxes(packed, 1, 2).reshape(2, -1)
    rows = packed[0].astype(jnp.int32)
    scales = packed[1]

    x = to_blocks(tokens, block)
    run = x.shape[0] // 2
    x_keep = lax.dynamic_slice_in_dim(x, core * run, run, axis=0)
    x_mate = swap_core(lax.dynamic_slice_in_dim(x, (1 - core) * run, run, axis=0))
    x_pair = jnp.where(core == 0, jnp.concatenate([x_keep, x_mate], axis=1),
                       jnp.concatenate([x_mate, x_keep], axis=1))
    x_all = jnp.concatenate([x_pair, swap_chip(x_pair)], axis=1)
    x_own = lax.all_gather(x_all, "tensor")
    x_mate = swap_core(x_own)
    x_parts = (x_own, x_mate)
    xt_parts = tuple(jnp.swapaxes(v, 2, 3) for v in x_parts)

    g = lax.all_gather(to_blocks(cotangent, block), "tensor", axis=0, tiled=True)
    g_chip = swap_chip(g)
    g_parts = (g, swap_core(g), g_chip, swap_core(g_chip))

    mate = swap_core(jnp.stack([lax.dynamic_slice_in_dim(w, (1 - core) * half, half, axis=1) for w in own]))
    first = part * per_part
    arrived, start, starts = {}, 0, []
    for j, size in enumerate(CHUNKS):
        mine = jnp.stack([lax.dynamic_slice_in_dim(w, core * half + first + start, size, axis=1) for w in own])
        send = jnp.concatenate([mine, lax.dynamic_slice_in_dim(mate, first + start, size, axis=2)], axis=1)
        arrived["a%d" % j] = swap_chip(send)
        arrived["b%d" % j] = swap_part(arrived["a%d" % j])
        starts.append(start)
        start += size

    me = jnp.reshape(core, (1,))
    carried = ()
    for n, names in enumerate(CALLS):
        half_cols = jnp.concatenate([
            (first if name[0] == "a" else per_part - first) + starts[int(name[1])]
            + jnp.arange(CHUNKS[int(name[1])], dtype=jnp.int32) for name in names])
        out = columns_call(n == 0, n == len(CALLS) - 1, tuple(CHUNKS[int(name[1])] for name in names),
                           core * half + half_cols, half_cols, rows, scales, me, own, mate,
                           [arrived[name] for name in names], x_parts, xt_parts, g_parts, carried)
        carried = (out[-1], *out[:4])
    *grads, grad_mate, keep, send = out
    grad_mate = swap_core(grad_mate)
    grads = [lax.dynamic_update_slice(v, grad_mate[m], (0, (1 - core) * half, 0, 0)) for m, v in enumerate(grads)]
    sums = (keep.astype(F32) + swap_core(send).astype(F32)).astype(BF16)
    sums = lax.psum_scatter(sums, "tensor", scatter_dimension=0, tiled=True)[0]
    layer_out, grad_tokens = (jnp.swapaxes(v, 0, 1).reshape(tokens.shape) for v in sums)
    return (layer_out, grad_tokens, *grads)


def local(*args):
    tokens, gate_values = args[0], args[2]
    paired = lax.axis_size("fsdp") == 4 and lax.axis_size("parts") == 2
    if paired and gate_values.shape[1] == 4 * sum(CHUNKS) and tokens.shape[1] % (2 * gate_values.shape[-1]) == 0:
        return local_pairs(*args)
    return local_gathered(*args)


def scaled_sum(products, factors):
    return jnp.sum(products * factors.astype(jnp.float32)[None, :, :, None], axis=1)


def slot_term(selected, grads, factors):
    return (
        jnp.einsum("tkra,trb->krab", selected, grads, preferred_element_type=jnp.float32)
        * factors[:, :, None, None]
    )


def local_gathered(
    tokens,
    cotangent,
    gate_values,
    gate_rows,
    gate_scale,
    up_values,
    up_rows,
    up_scale,
    down_values,
    down_cols,
    down_scale,
):
    block_size = gate_values.shape[-1]
    token_count = tokens.shape[0]
    tensor_count = lax.axis_size("tensor")
    nblocks = tokens.shape[1] * tensor_count // block_size
    local_blocks = nblocks // tensor_count
    gathered = lax.all_gather(tokens, "tensor", axis=1, tiled=True)
    x_blocks = gathered.reshape(token_count, nblocks, block_size)
    gate_where, up_where, down_where = (
        lax.all_gather(gate_rows, "fsdp", axis=0, tiled=True),
        lax.all_gather(up_rows, "fsdp", axis=0, tiled=True),
        lax.all_gather(down_cols, "fsdp", axis=0, tiled=True),
    )
    gate_blocks, gate_factor, up_blocks, up_factor, down_blocks, down_factor = (
        lax.all_gather(gate_values, "fsdp", axis=0, tiled=True),
        lax.all_gather(gate_scale, "fsdp", axis=0, tiled=True),
        lax.all_gather(up_values, "fsdp", axis=0, tiled=True),
        lax.all_gather(up_scale, "fsdp", axis=0, tiled=True),
        lax.all_gather(down_values, "fsdp", axis=0, tiled=True),
        lax.all_gather(down_scale, "fsdp", axis=0, tiled=True),
    )
    gate_sel = x_blocks[:, gate_where]
    up_sel = x_blocks[:, up_where]
    gate_pre = scaled_sum(
        jnp.einsum("tkra,krab->tkrb", gate_sel, gate_blocks, preferred_element_type=jnp.float32),
        gate_factor,
    )
    up_pre = scaled_sum(
        jnp.einsum("tkra,krab->tkrb", up_sel, up_blocks, preferred_element_type=jnp.float32),
        up_factor,
    )
    sigmoid_gate = jax.nn.sigmoid(gate_pre)
    activated = gate_pre * sigmoid_gate
    hidden = (activated * up_pre).astype(jnp.bfloat16)
    down_float = down_factor.astype(jnp.float32)
    down_scaled = (
        jnp.einsum("trb,krbc->krtc", hidden, down_blocks, preferred_element_type=jnp.float32)
        * down_float[:, :, None, None]
    )
    out_full = (
        jnp.zeros((nblocks, token_count, block_size), jnp.float32).at[down_where].add(down_scaled)
    )
    out_part = lax.psum_scatter(
        out_full.astype(jnp.bfloat16), "tensor", scatter_dimension=0, tiled=True
    ).astype(jnp.float32)
    layer_out = (
        jnp.transpose(out_part, (1, 0, 2))
        .reshape(token_count, local_blocks * block_size)
        .astype(jnp.bfloat16)
    )
    grad_full = lax.all_gather(cotangent, "tensor", axis=1, tiled=True).reshape(
        token_count, nblocks, block_size
    )
    down_sel = grad_full[:, down_where]
    gate_float = gate_factor.astype(jnp.float32)
    up_float = up_factor.astype(jnp.float32)
    grad_hidden = scaled_sum(
        jnp.einsum("tkrc,krbc->tkrb", down_sel, down_blocks, preferred_element_type=jnp.float32),
        down_factor,
    )
    grad_down = lax.psum_scatter(
        (
            jnp.einsum("trb,tkrc->krbc", hidden, down_sel, preferred_element_type=jnp.float32)
            * down_float[:, :, None, None]
        ).astype(jnp.bfloat16),
        "fsdp",
        scatter_dimension=0,
        tiled=True,
    )
    grad_gate_act = (
        grad_hidden * up_pre * sigmoid_gate * (1.0 + gate_pre * (1.0 - sigmoid_gate))
    ).astype(jnp.bfloat16)
    grad_up_act = (grad_hidden * activated).astype(jnp.bfloat16)
    grad_gate = lax.psum_scatter(
        slot_term(gate_sel, grad_gate_act, gate_float).astype(jnp.bfloat16),
        "fsdp",
        scatter_dimension=0,
        tiled=True,
    )
    grad_up = lax.psum_scatter(
        slot_term(up_sel, grad_up_act, up_float).astype(jnp.bfloat16),
        "fsdp",
        scatter_dimension=0,
        tiled=True,
    )
    back_gate = (
        jnp.einsum("trb,krab->krta", grad_gate_act, gate_blocks, preferred_element_type=jnp.float32)
        * gate_float[:, :, None, None]
    )
    back_up = (
        jnp.einsum("trb,krab->krta", grad_up_act, up_blocks, preferred_element_type=jnp.float32)
        * up_float[:, :, None, None]
    )
    in_full = (
        jnp.zeros((nblocks, token_count, block_size), jnp.float32)
        .at[gate_where]
        .add(back_gate)
        .at[up_where]
        .add(back_up)
    )
    in_part = lax.psum_scatter(
        in_full.astype(jnp.bfloat16), "tensor", scatter_dimension=0, tiled=True
    ).astype(jnp.float32)
    grad_tokens = (
        jnp.transpose(in_part, (1, 0, 2))
        .reshape(token_count, local_blocks * block_size)
        .astype(jnp.bfloat16)
    )
    return (layer_out, grad_tokens, grad_gate, grad_up, grad_down)


def solution(mesh):
    in_specs = (
        P(("parts", "fsdp"), "tensor"),
        P(("parts", "fsdp"), "tensor"),
        P("fsdp", "tensor", None, None),
        P("fsdp", "tensor"),
        P("fsdp", "tensor"),
        P("fsdp", "tensor", None, None),
        P("fsdp", "tensor"),
        P("fsdp", "tensor"),
        P("fsdp", "tensor", None, None),
        P("fsdp", "tensor"),
        P("fsdp", "tensor"),
    )
    out_specs = (
        P(("parts", "fsdp"), "tensor"),
        P(("parts", "fsdp"), "tensor"),
        P(("parts", "fsdp"), "tensor", None, None),
        P(("parts", "fsdp"), "tensor", None, None),
        P(("parts", "fsdp"), "tensor", None, None),
    )
    return jax.shard_map(local, mesh=mesh, in_specs=in_specs, out_specs=out_specs, check_vma=False)
```

```python
import functools

import jax
import jax.numpy as jnp
from jax import lax
from jax.experimental import pallas as pl
from jax.experimental.pallas import tpu as pltpu
from jax.sharding import PartitionSpec as P

F32, BF16 = jnp.float32, jnp.bfloat16
ANY = pl.BlockSpec(memory_space=pl.ANY)
SMEM = pl.BlockSpec(memory_space=pltpu.SMEM)
PARAMS = pltpu.CompilerParams(vmem_limit_bytes=50 * 2**20)
STEP = 2


def dot(a, b, ca, cb):
    return lax.dot_general(a, b, (((ca,), (cb,)), ((), ())), preferred_element_type=F32)


def over_columns(n, step, body):
    if n // step:

        def run(j, _):
            body([j * step + u for u in range(step)])
            return 0

        lax.fori_loop(0, n // step, run, 0)
    if n % step:
        body([n - n % step + u for u in range(n % step)])


def token_copies(core, parts, full, sem):
    out = []
    rest = full.shape[1] // 4
    for where, part in ((core, parts[0]), (1 - core, parts[1])):
        for chip in range(2):
            at = pl.ds(pl.multiple_of((2 * chip + where) * rest, rest), rest)
            out.append(pltpu.make_async_copy(part.at[:, pl.ds(chip * rest, rest), :], full.at[:, at, :], sem))
    return out


def weight_copies(sizes, half_cols, base, own, mate, others, own_s, mate_s, other_s, sems):
    out = []
    start = 0
    for size, other in zip(sizes, others):

        def of(i, start=start, other=other):
            h = half_cols[i]
            sem = sems.at[i]
            copies = [pltpu.make_async_copy(w.at[:, base + h], own_s.at[i, m], sem) for m, w in enumerate(own)]
            copies.append(pltpu.make_async_copy(mate.at[:, :, h], mate_s.at[i], sem))
            copies.append(pltpu.make_async_copy(other.at[:, :, i - start], other_s.at[i], sem))
            return copies

        out.append((start, size, of))
        start += size
    return out


def start_weights(copies):
    for start, size, of in copies:

        def go(i, _, of=of):
            for c in of(i):
                c.start()
            return 0

        lax.fori_loop(start, start + size, go, 0)


def scaled(own_s, mate_s, other_s, scale, i, m):
    count = own_s.shape[2]
    blocks = [own_s[i, m, k] for k in range(count)] + [mate_s[i, m, k] for k in range(count)]
    blocks += [other_s[i, m, k] for k in range(2 * count)]
    return [b * scale(m, k).astype(BF16) for k, b in enumerate(blocks)]


def wait_weights(own_s, mate_s, other_s, sems, i):
    for ref in (own_s, mate_s, other_s):
        pltpu.make_async_copy(ref.at[i], ref.at[i], sems.at[i]).wait()


def picker(rows, scales, h, slots):
    return (lambda m, k: rows[h * 3 * slots + m * slots + k]), (lambda m, k: scales[h * 3 * slots + m * slots + k])


def forward_kernel(first, sizes, slots, *refs):
    refs = list(refs)
    take = lambda n: [refs.pop(0) for _ in range(n)]
    half_cols, rows, scales, me = take(4)
    own = take(3)
    (mate,) = take(1)
    others = take(len(sizes))
    x_parts = take(2)
    if not first:
        sums_in, _ = take(2)
    sums_out, acts = take(2)
    x_s, acc, own_s, mate_s, other_s, act_s, wsems, asems, sems = refs
    n = sum(sizes)
    core = me[0]
    copies = token_copies(core, x_parts, x_s, sems.at[0])
    for c in copies:
        c.start()
    start_weights(weight_copies(sizes, half_cols, me[1], own, mate, others, own_s, mate_s, other_s, wsems))
    if first:
        acc[...] = jnp.zeros(acc.shape, F32)
    else:
        sums = pltpu.make_async_copy(sums_in, acc, sems.at[1])
        sums.start()
        sums.wait()
    for c in copies:
        c.wait()
    mine = x_s.shape[1] // 2
    block = x_s.shape[2]

    def body(columns):
        for i in columns:
            wait_weights(own_s, mate_s, other_s, wsems, i)
        kept = []
        for i in columns:
            row, scale = picker(rows, scales, half_cols[i], slots)
            weights = functools.partial(scaled, own_s, mate_s, other_s, scale, i)
            pre = []
            for m in range(2):
                selected = jnp.concatenate([x_s[row(m, k)] for k in range(slots)], axis=1)
                pre.append(dot(selected, jnp.concatenate(weights(m), axis=0), 1, 0))
            gate_pre, up_pre = pre
            s = jax.nn.sigmoid(gate_pre)
            activated = gate_pre * s
            hidden = (activated * up_pre).astype(BF16)
            act_s[i, 0] = hidden
            act_s[i, 1] = (up_pre * s * (1.0 + gate_pre * (1.0 - s))).astype(BF16)
            act_s[i, 2] = activated.astype(BF16)
            pltpu.make_async_copy(act_s.at[i], acts.at[half_cols[i]], asems.at[i]).start()
            kept.append((row, dot(hidden[:mine], jnp.concatenate(weights(2), axis=1), 1, 0)))
        for row, out in kept:
            for k in range(slots):
                acc[row(2, k)] += out[:, k * block : (k + 1) * block]

    over_columns(n, STEP, body)
    sums = pltpu.make_async_copy(acc, sums_out, sems.at[1])
    sums.start()

    def finish(i, _):
        pltpu.make_async_copy(act_s.at[i], acts.at[half_cols[i]], asems.at[i]).wait()
        return 0

    lax.fori_loop(0, n, finish, 0)
    sums.wait()


def backward_kernel(first, sizes, slots, *refs):
    refs = list(refs)
    take = lambda n: [refs.pop(0) for _ in range(n)]
    half_cols, rows, scales, me = take(4)
    own = take(3)
    (mate,) = take(1)
    others = take(len(sizes))
    g_parts = take(2)
    (acts_in,) = take(1)
    if not first:
        (sums_in,) = take(1)
    sums_out, acts = take(2)
    g_s, acc, own_s, mate_s, other_s, act_s, wsems, asems, sems = refs
    n = sum(sizes)
    core = me[0]
    copies = token_copies(core, g_parts, g_s, sems.at[0])
    for c in copies:
        c.start()
    start_weights(weight_copies(sizes, half_cols, me[1], own, mate, others, own_s, mate_s, other_s, wsems))

    def derivatives(i, away=False):
        here, there = act_s.at[i, pl.ds(1, 2)], acts.at[half_cols[i], pl.ds(1, 2)]
        return pltpu.make_async_copy(here, there, asems.at[i]) if away else pltpu.make_async_copy(there, here, asems.at[i])

    def fetch(i, _):
        derivatives(i).start()
        return 0

    lax.fori_loop(0, n, fetch, 0)
    if first:
        acc[...] = jnp.zeros(acc.shape, F32)
    else:
        sums = pltpu.make_async_copy(sums_in, acc, sems.at[1])
        sums.start()
        sums.wait()
    for c in copies:
        c.wait()
    mine = g_s.shape[1] // 2
    block = g_s.shape[2]

    def body(columns):
        for i in columns:
            wait_weights(own_s, mate_s, other_s, wsems, i)
            derivatives(i).wait()
        kept = []
        for i in columns:
            row, scale = picker(rows, scales, half_cols[i], slots)
            weights = functools.partial(scaled, own_s, mate_s, other_s, scale, i)
            selected = jnp.concatenate([g_s[row(2, k)] for k in range(slots)], axis=1)
            grad_hidden = dot(selected, jnp.concatenate(weights(2), axis=1), 1, 1)
            for m in range(2):
                act = (grad_hidden * act_s[i, 1 + m].astype(F32)).astype(BF16)
                act_s[i, 1 + m] = act
                kept.append((row, m, dot(act[:mine], jnp.concatenate(weights(m), axis=0), 1, 1)))
            derivatives(i, True).start()
        for row, m, back in kept:
            for k in range(slots):
                acc[row(m, k)] += back[:, k * block : (k + 1) * block]

    over_columns(n, STEP, body)
    sums = pltpu.make_async_copy(acc, sums_out, sems.at[1])
    sums.start()

    def finish(i, _):
        derivatives(i, True).wait()
        return 0

    lax.fori_loop(0, n, finish, 0)
    sums.wait()


def columns_call(backward, first, sizes, half_cols, rows, scales, me, own, mate, others, token_parts, sums, acts):
    own_slots, _, block, _ = own[0].shape
    n = sum(sizes)
    nblocks, half_tokens, _ = token_parts[0].shape
    tokens = 2 * half_tokens
    args = [half_cols, rows, scales, me, *own, mate, *others, *token_parts]
    in_specs = [SMEM] * 4 + [ANY] * (len(args) - 4)
    aliases = {}
    more = ([acts] if first else [acts, sums]) if backward else ([] if first else [sums, acts])
    for v in more:
        aliases[len(args)] = 0 if v is sums else 1
        args.append(v)
        in_specs.append(ANY)
    kernel = backward_kernel if backward else forward_kernel
    return pl.pallas_call(
        functools.partial(kernel, first, sizes, 4 * own_slots),
        in_specs=in_specs,
        out_specs=[ANY, ANY],
        out_shape=[jax.ShapeDtypeStruct((nblocks, half_tokens, block), F32),
                   jax.ShapeDtypeStruct((mate.shape[2], 3, tokens, block), BF16)],
        scratch_shapes=[
            pltpu.VMEM((nblocks, tokens, block), BF16),
            pltpu.VMEM((nblocks, half_tokens, block), F32),
            pltpu.VMEM((n, 3, own_slots, block, block), BF16),
            pltpu.VMEM((n, 3, own_slots, block, block), BF16),
            pltpu.VMEM((n, 3, 2 * own_slots, block, block), BF16),
            pltpu.VMEM((n, 3, tokens, block), BF16),
            pltpu.SemaphoreType.DMA((n,)),
            pltpu.SemaphoreType.DMA((n,)),
            pltpu.SemaphoreType.DMA((2,)),
        ],
        input_output_aliases=aliases,
        compiler_params=PARAMS,
        name="backward" if backward else "forward",
    )(*args)


def gradients_kernel(own_slots, slots, rows, scales, me, x_own, x_mate, g_own, g_mate, acts,
                     grad_gate, grad_up, grad_down, grad_mate, x_s, g_s, act_s, out_s, asems, osems, sems):
    core = me[0]
    n = acts.shape[0]
    depth = act_s.shape[0]
    x_copies = token_copies(core, (x_own, x_mate), x_s, sems.at[0])
    g_copies = token_copies(core, (g_own, g_mate), g_s, sems.at[1])
    for c in x_copies + g_copies:
        c.start()
    grads = (grad_gate, grad_up, grad_down)
    block = x_s.shape[2]
    half = 2 * own_slots

    def fetch(i):
        return pltpu.make_async_copy(acts.at[i], act_s.at[lax.rem(i, depth)], asems.at[lax.rem(i, depth)])

    def stores(i):
        at = lax.rem(i, depth)
        out = [pltpu.make_async_copy(out_s.at[at, m, pl.ds(0, own_slots)], v.at[:, me[1] + i], osems.at[at]) for m, v in enumerate(grads)]
        out.append(pltpu.make_async_copy(out_s.at[at, :, pl.ds(own_slots, own_slots)], grad_mate.at[:, :, i], osems.at[at]))
        return out

    for i in range(depth):
        fetch(i).start()
    for c in x_copies + g_copies:
        c.wait()

    def body(columns):
        for i in columns:
            fetch(i).wait()

            @pl.when(i >= depth)
            def _():
                for c in stores(i - depth):
                    c.wait()

        for i in columns:
            at = lax.rem(i, depth)
            row, scale = picker(rows, scales, i, slots)
            for m, source in ((0, x_s), (1, x_s), (2, g_s)):
                act = act_s[at, (m + 1) % 3]
                selected = jnp.concatenate([source[row(m, k)] for k in range(half)], axis=1)
                out = dot(act, selected, 0, 0)
                for k in range(half):
                    piece = (out[:, k * block : (k + 1) * block] * scale(m, k)).astype(BF16)
                    out_s[at, m, k] = piece if m == 2 else piece.T
        for i in columns:
            for c in stores(i):
                c.start()

            @pl.when(i + depth < n)
            def _():
                fetch(i + depth).start()

    over_columns(n, STEP, body)
    for i in range(n - depth, n):
        for c in stores(i):
            c.wait()


def gradients_call(rows, scales, me, x_parts, g_parts, acts, own_slots, columns):
    n, _, tokens, block = acts.shape
    nblocks = x_parts[0].shape[0]
    depth = min(4, n)
    grad = jax.ShapeDtypeStruct((own_slots, columns, block, block), BF16)
    return pl.pallas_call(
        functools.partial(gradients_kernel, own_slots, 4 * own_slots),
        in_specs=[SMEM] * 3 + [ANY] * 5,
        out_specs=[ANY] * 4,
        out_shape=[grad] * 3 + [jax.ShapeDtypeStruct((3, own_slots, n, block, block), BF16)],
        scratch_shapes=[
            pltpu.VMEM((nblocks, tokens, block), BF16),
            pltpu.VMEM((nblocks, tokens, block), BF16),
            pltpu.VMEM((depth, 3, tokens, block), BF16),
            pltpu.VMEM((depth, 3, 2 * own_slots, block, block), BF16),
            pltpu.SemaphoreType.DMA((depth,)),
            pltpu.SemaphoreType.DMA((depth,)),
            pltpu.SemaphoreType.DMA((2,)),
        ],
        compiler_params=PARAMS,
        name="gradients",
    )(rows, scales, me, *x_parts, *g_parts, acts)


def copy_kernel(pairs_of, n_in, *refs):
    me, sem = refs[0], refs[-1]
    copies = [pltpu.make_async_copy(a, b, sem) for a, b in pairs_of(me, refs[1 : 1 + n_in], refs[1 + n_in : -1])]
    for c in copies:
        c.start()
    for c in copies:
        c.wait()


def copies_call(name, pairs_of, me, args, shapes):
    return pl.pallas_call(
        functools.partial(copy_kernel, pairs_of, len(args)),
        in_specs=[SMEM] + [ANY] * len(args),
        out_specs=[ANY] * len(shapes),
        out_shape=[jax.ShapeDtypeStruct(s, BF16) for s in shapes],
        scratch_shapes=[pltpu.SemaphoreType.DMA],
        compiler_params=PARAMS,
        name=name,
    )(me, *args)


def to_blocks(v, block):
    return jnp.swapaxes(v.reshape(v.shape[0], -1, block), 0, 1)


def chunk_sizes(count):
    twos = (count - 2) // 2
    return [2] * twos + [1] * (count - 2 * twos)


def local_pairs(tokens, cotangent, gate_values, gate_rows, gate_scale, up_values, up_rows, up_scale,
                down_values, down_cols, down_scale):
    own = (gate_values, up_values, down_values)
    own_slots, columns, block, _ = gate_values.shape
    half = columns // 2
    per_part = half // 2
    core = lax.rem(lax.axis_index("fsdp"), 2)
    part = lax.axis_index("parts")
    first = part * per_part
    swap_core = lambda v: lax.ppermute(v, "fsdp", [(i, i ^ 1) for i in range(4)])
    swap_chip = lambda v: lax.ppermute(v, "fsdp", [(i, i ^ 2) for i in range(4)])
    swap_part = lambda v: lax.ppermute(v, "parts", [(0, 1), (1, 0)])
    after = lambda v, earlier: lax.optimization_barrier((v, earlier))[0]
    me = jnp.stack([core, core * half, (1 - core) * half, first])

    packed = jnp.stack([v.astype(F32) for v in (gate_rows, up_rows, down_cols, gate_scale, up_scale, down_scale)])
    packed = jnp.concatenate([packed, swap_core(packed)], axis=1)
    packed = jnp.concatenate([packed, swap_chip(packed)], axis=1)
    packed = lax.dynamic_slice_in_dim(packed, core * half, half, axis=2)
    packed = jnp.transpose(packed.reshape(2, 3, -1, half), (0, 3, 1, 2)).reshape(2, -1)
    rows = packed[0].astype(jnp.int32)
    scales = packed[1]

    x = to_blocks(tokens, block)
    g = to_blocks(cotangent, block)
    x_chip = swap_chip(x)
    g_chip = swap_chip(g)
    x_own = lax.all_gather(jnp.concatenate([x, x_chip], axis=1), "tensor", axis=0, tiled=True)
    g_pair = after(jnp.concatenate([g, g_chip], axis=1), x_own)
    g_own = lax.all_gather(g_pair, "tensor", axis=0, tiled=True)
    x_parts = (x_own, swap_core(x_own))
    g_parts = (g_own, swap_core(g_own))

    def mate_pairs(me, ins, outs):
        return [(w.at[:, pl.ds(me[2], half)], outs[0].at[m]) for m, w in enumerate(ins)]

    mate = swap_core(copies_call("mate_blocks", mate_pairs, me, own, [(3, own_slots, half, block, block)])[0])
    sizes = chunk_sizes(per_part)
    starts = [sum(sizes[:j]) for j in range(len(sizes))]

    def chunk_pairs(me, ins, outs):
        out = []
        for at, size, dst in zip(starts, sizes, outs):
            out += [(w.at[:, pl.ds(me[1] + me[3] + at, size)], dst.at[m, pl.ds(0, own_slots)]) for m, w in enumerate(ins[:3])]
            out.append((ins[3].at[:, :, pl.ds(me[3] + at, size)], dst.at[:, pl.ds(own_slots, own_slots)]))
        return out

    sends = copies_call("chunk_blocks", chunk_pairs, me, (*own, mate), [(3, 2 * own_slots, n, block, block) for n in sizes])
    direct, relayed = [], []
    for j, send in enumerate(sends):
        direct.append(swap_chip(after(send, direct[j - 2] if j >= 2 else (x_chip, g_chip)[j])))
        relayed.append(swap_part(direct[j]))

    def column_ids(name):
        j = int(name[1:])
        return (first if name[0] == "a" else per_part - first) + starts[j] + jnp.arange(sizes[j], dtype=jnp.int32)

    def call(backward, names, sums, acts):
        half_cols = jnp.concatenate([column_ids(name) for name in names])
        others = [(direct if name[0] == "a" else relayed)[int(name[1:])] for name in names]
        return columns_call(backward, sums is None, tuple(sizes[int(name[1:])] for name in names), half_cols, rows, scales,
                            me, own, mate, others, g_parts if backward else x_parts, sums, acts)

    count = len(sizes)
    order = ["a0"] + [v for j in range(1, count) for v in ("a%d" % j, "b%d" % (j - 1))] + ["b%d" % (count - 1)]
    groups = (order[:5], order[5:7], order[7:])
    outs, acts = call(False, groups[0], None, None)
    outs, acts = call(False, groups[1], outs, acts)
    ins, acts = call(True, groups[0] + groups[1], None, acts)
    outs, acts = call(False, groups[2], outs, acts)
    ins, acts = call(True, groups[2], ins, acts)

    rest = tokens.shape[0]

    def reduced(sums):
        keep = lax.dynamic_slice_in_dim(sums, core * rest, rest, axis=1)
        send = lax.dynamic_slice_in_dim(sums, (1 - core) * rest, rest, axis=1).astype(BF16)
        sums = (keep + swap_core(send).astype(F32)).astype(BF16)
        sums = lax.psum_scatter(sums, "tensor", scatter_dimension=0, tiled=True)
        return jnp.swapaxes(sums, 0, 1).reshape(tokens.shape)

    layer_out, grad_tokens = reduced(outs), reduced(ins)

    *grads, grad_mate = gradients_call(rows, scales, me, x_parts, g_parts, acts, own_slots, columns)
    grad_mate = swap_core(grad_mate)
    grads = [lax.dynamic_update_slice(v, grad_mate[m], (0, (1 - core) * half, 0, 0)) for m, v in enumerate(grads)]
    return (layer_out, grad_tokens, *grads)


def scaled_sum(products, factors):
    return jnp.sum(products * factors.astype(jnp.float32)[None, :, :, None], axis=1)


def slot_term(selected, grads, factors):
    return (
        jnp.einsum("tkra,trb->krab", selected, grads, preferred_element_type=jnp.float32)
        * factors[:, :, None, None]
    )


def local_gathered(
    tokens,
    cotangent,
    gate_values,
    gate_rows,
    gate_scale,
    up_values,
    up_rows,
    up_scale,
    down_values,
    down_cols,
    down_scale,
):
    block_size = gate_values.shape[-1]
    token_count = tokens.shape[0]
    tensor_count = lax.axis_size("tensor")
    nblocks = tokens.shape[1] * tensor_count // block_size
    local_blocks = nblocks // tensor_count
    gathered = lax.all_gather(tokens, "tensor", axis=1, tiled=True)
    x_blocks = gathered.reshape(token_count, nblocks, block_size)
    gate_where, up_where, down_where = (
        lax.all_gather(gate_rows, "fsdp", axis=0, tiled=True),
        lax.all_gather(up_rows, "fsdp", axis=0, tiled=True),
        lax.all_gather(down_cols, "fsdp", axis=0, tiled=True),
    )
    gate_blocks, gate_factor, up_blocks, up_factor, down_blocks, down_factor = (
        lax.all_gather(gate_values, "fsdp", axis=0, tiled=True),
        lax.all_gather(gate_scale, "fsdp", axis=0, tiled=True),
        lax.all_gather(up_values, "fsdp", axis=0, tiled=True),
        lax.all_gather(up_scale, "fsdp", axis=0, tiled=True),
        lax.all_gather(down_values, "fsdp", axis=0, tiled=True),
        lax.all_gather(down_scale, "fsdp", axis=0, tiled=True),
    )
    gate_sel = x_blocks[:, gate_where]
    up_sel = x_blocks[:, up_where]
    gate_pre = scaled_sum(
        jnp.einsum("tkra,krab->tkrb", gate_sel, gate_blocks, preferred_element_type=jnp.float32),
        gate_factor,
    )
    up_pre = scaled_sum(
        jnp.einsum("tkra,krab->tkrb", up_sel, up_blocks, preferred_element_type=jnp.float32),
        up_factor,
    )
    sigmoid_gate = jax.nn.sigmoid(gate_pre)
    activated = gate_pre * sigmoid_gate
    hidden = (activated * up_pre).astype(jnp.bfloat16)
    down_float = down_factor.astype(jnp.float32)
    down_scaled = (
        jnp.einsum("trb,krbc->krtc", hidden, down_blocks, preferred_element_type=jnp.float32)
        * down_float[:, :, None, None]
    )
    out_full = (
        jnp.zeros((nblocks, token_count, block_size), jnp.float32).at[down_where].add(down_scaled)
    )
    out_part = lax.psum_scatter(
        out_full.astype(jnp.bfloat16), "tensor", scatter_dimension=0, tiled=True
    ).astype(jnp.float32)
    layer_out = (
        jnp.transpose(out_part, (1, 0, 2))
        .reshape(token_count, local_blocks * block_size)
        .astype(jnp.bfloat16)
    )
    grad_full = lax.all_gather(cotangent, "tensor", axis=1, tiled=True).reshape(
        token_count, nblocks, block_size
    )
    down_sel = grad_full[:, down_where]
    gate_float = gate_factor.astype(jnp.float32)
    up_float = up_factor.astype(jnp.float32)
    grad_hidden = scaled_sum(
        jnp.einsum("tkrc,krbc->tkrb", down_sel, down_blocks, preferred_element_type=jnp.float32),
        down_factor,
    )
    grad_down = lax.psum_scatter(
        (
            jnp.einsum("trb,tkrc->krbc", hidden, down_sel, preferred_element_type=jnp.float32)
            * down_float[:, :, None, None]
        ).astype(jnp.bfloat16),
        "fsdp",
        scatter_dimension=0,
        tiled=True,
    )
    grad_gate_act = (
        grad_hidden * up_pre * sigmoid_gate * (1.0 + gate_pre * (1.0 - sigmoid_gate))
    ).astype(jnp.bfloat16)
    grad_up_act = (grad_hidden * activated).astype(jnp.bfloat16)
    grad_gate = lax.psum_scatter(
        slot_term(gate_sel, grad_gate_act, gate_float).astype(jnp.bfloat16),
        "fsdp",
        scatter_dimension=0,
        tiled=True,
    )
    grad_up = lax.psum_scatter(
        slot_term(up_sel, grad_up_act, up_float).astype(jnp.bfloat16),
        "fsdp",
        scatter_dimension=0,
        tiled=True,
    )
    back_gate = (
        jnp.einsum("trb,krab->krta", grad_gate_act, gate_blocks, preferred_element_type=jnp.float32)
        * gate_float[:, :, None, None]
    )
    back_up = (
        jnp.einsum("trb,krab->krta", grad_up_act, up_blocks, preferred_element_type=jnp.float32)
        * up_float[:, :, None, None]
    )
    in_full = (
        jnp.zeros((nblocks, token_count, block_size), jnp.float32)
        .at[gate_where]
        .add(back_gate)
        .at[up_where]
        .add(back_up)
    )
    in_part = lax.psum_scatter(
        in_full.astype(jnp.bfloat16), "tensor", scatter_dimension=0, tiled=True
    ).astype(jnp.float32)
    grad_tokens = (
        jnp.transpose(in_part, (1, 0, 2))
        .reshape(token_count, local_blocks * block_size)
        .astype(jnp.bfloat16)
    )
    return (layer_out, grad_tokens, grad_gate, grad_up, grad_down)


def local(*args):
    tokens, gate_values = args[0], args[2]
    paired = lax.axis_size("fsdp") == 4 and lax.axis_size("parts") == 2
    if paired and gate_values.shape[1] % 4 == 0 and gate_values.shape[1] >= 16:
        return local_pairs(*args)
    return local_gathered(*args)


def solution(mesh):
    in_specs = (
        P(("parts", "fsdp"), "tensor"),
        P(("parts", "fsdp"), "tensor"),
        P("fsdp", "tensor", None, None),
        P("fsdp", "tensor"),
        P("fsdp", "tensor"),
        P("fsdp", "tensor", None, None),
        P("fsdp", "tensor"),
        P("fsdp", "tensor"),
        P("fsdp", "tensor", None, None),
        P("fsdp", "tensor"),
        P("fsdp", "tensor"),
    )
    out_specs = (
        P(("parts", "fsdp"), "tensor"),
        P(("parts", "fsdp"), "tensor"),
        P(("parts", "fsdp"), "tensor", None, None),
        P(("parts", "fsdp"), "tensor", None, None),
        P(("parts", "fsdp"), "tensor", None, None),
    )
    return jax.shard_map(local, mesh=mesh, in_specs=in_specs, out_specs=out_specs, check_vma=False)
```

```python
import functools

import jax
import jax.numpy as jnp
from jax import lax
from jax.experimental import pallas as pl
from jax.experimental.pallas import tpu as pltpu
from jax.sharding import PartitionSpec as P

F32, BF16 = jnp.float32, jnp.bfloat16
ANY = pl.BlockSpec(memory_space=pl.ANY)
HBM = pl.BlockSpec(memory_space=pltpu.HBM)
SMEM = pl.BlockSpec(memory_space=pltpu.SMEM)
PARAMS = pltpu.CompilerParams(vmem_limit_bytes=50 * 2**20)
STEP = 2


def dot(a, b, ca, cb):
    return lax.dot_general(a, b, (((ca,), (cb,)), ((), ())), preferred_element_type=F32)


def estimate(us):
    return pl.CostEstimate(flops=int(us * 1.1e9), bytes_accessed=int(us * 3.0e6), transcendentals=0)


def over_columns(n, step, body):
    if n // step:

        def run(j, _):
            body([j * step + u for u in range(step)])
            return 0

        lax.fori_loop(0, n // step, run, 0)
    if n % step:
        body([n - n % step + u for u in range(n % step)])


def token_copies(me, parts, which, full, sem):
    out = []
    rest = full.shape[1] // 4
    for core, part in zip((me[0], 1 - me[0]), parts):
        shards, run = part.shape[0], part.shape[1] // 2
        for shard in range(shards):
            for chip in range(2):
                here = part.at[shard, pl.ds(which * run, run), pl.ds(chip * rest, rest), :]
                to = full.at[pl.ds(shard * run, run), pl.ds(pl.multiple_of((2 * chip + core) * rest, rest), rest), :]
                out.append(pltpu.make_async_copy(here, to, sem))
    return out


def weight_copies(sizes, half_cols, base, own, mate, others, own_s, mate_s, other_s, sems):
    out = []
    start = 0
    for size, other in zip(sizes, others):

        def of(i, start=start, other=other):
            h = half_cols[i]
            sem = sems.at[i]
            copies = [pltpu.make_async_copy(w.at[:, base + h], own_s.at[i, m], sem) for m, w in enumerate(own)]
            copies.append(pltpu.make_async_copy(mate.at[:, :, h], mate_s.at[i], sem))
            copies.append(pltpu.make_async_copy(other.at[:, :, i - start], other_s.at[i], sem))
            return copies

        out.append((start, size, of))
        start += size
    return out


def start_weights(copies):
    for start, size, of in copies:

        def go(i, _, of=of):
            for c in of(i):
                c.start()
            return 0

        lax.fori_loop(start, start + size, go, 0)


def scaled(own_s, mate_s, other_s, scale, i, m):
    count = own_s.shape[2]
    blocks = [own_s[i, m, k] for k in range(count)] + [mate_s[i, m, k] for k in range(count)]
    blocks += [other_s[i, m, k] for k in range(2 * count)]
    return [b * scale(m, k).astype(BF16) for k, b in enumerate(blocks)]


def wait_weights(own_s, mate_s, other_s, sems, i):
    for ref in (own_s, mate_s, other_s):
        pltpu.make_async_copy(ref.at[i], ref.at[i], sems.at[i]).wait()


def picker(rows, scales, h, slots):
    return (lambda m, k: rows[h * 3 * slots + m * slots + k]), (lambda m, k: scales[h * 3 * slots + m * slots + k])


def hand_out(core, acc, stage, sums_out, sems):
    if len(sums_out) == 1:
        copies = [pltpu.make_async_copy(acc, sums_out[0], sems.at[1])]
    else:
        rest = acc.shape[1] // 2
        mine, other = (pl.ds(pl.multiple_of(c * rest, rest), rest) for c in (core, 1 - core))
        stage[...] = acc[:, other, :].astype(BF16)
        copies = [pltpu.make_async_copy(stage, sums_out[1], sems.at[0]), pltpu.make_async_copy(acc.at[:, mine, :], sums_out[0], sems.at[1])]
    for c in copies:
        c.start()
    return copies


def forward_kernel(first, last, sizes, slots, parts, *refs):
    refs = list(refs)
    take = lambda n: [refs.pop(0) for _ in range(n)]
    _, half_cols, rows, scales, me = take(5)
    own = take(3)
    (mate,) = take(1)
    others = take(len(sizes))
    x_parts = take(parts)
    if not first:
        sums_in, _ = take(2)
    *sums_out, acts = take(3 if last else 2)
    x_s, acc, own_s, mate_s, other_s, act_s, stage, wsems, asems, sems = refs
    n = sum(sizes)
    copies = token_copies(me, x_parts, 0, x_s, sems.at[0])
    for c in copies:
        c.start()
    start_weights(weight_copies(sizes, half_cols, me[1], own, mate, others, own_s, mate_s, other_s, wsems))
    if first:
        acc[...] = jnp.zeros(acc.shape, F32)
    else:
        sums = pltpu.make_async_copy(sums_in, acc, sems.at[1])
        sums.start()
        sums.wait()
    for c in copies:
        c.wait()
    mine = x_s.shape[1] // 2
    block = x_s.shape[2]

    def body(columns):
        for i in columns:
            wait_weights(own_s, mate_s, other_s, wsems, i)
        kept = []
        for i in columns:
            row, scale = picker(rows, scales, half_cols[i], slots)
            weights = functools.partial(scaled, own_s, mate_s, other_s, scale, i)
            pre = []
            for m in range(2):
                selected = jnp.concatenate([x_s[row(m, k)] for k in range(slots)], axis=1)
                pre.append(dot(selected, jnp.concatenate(weights(m), axis=0), 1, 0))
            gate_pre, up_pre = pre
            s = jax.nn.sigmoid(gate_pre)
            activated = gate_pre * s
            hidden = (activated * up_pre).astype(BF16)
            act_s[i, 0] = hidden
            act_s[i, 1] = (up_pre * s * (1.0 + gate_pre * (1.0 - s))).astype(BF16)
            act_s[i, 2] = activated.astype(BF16)
            pltpu.make_async_copy(act_s.at[i], acts.at[half_cols[i]], asems.at[i]).start()
            kept.append((row, dot(hidden[:mine], jnp.concatenate(weights(2), axis=1), 1, 0)))
        for row, out in kept:
            for k in range(slots):
                acc[row(2, k)] += out[:, k * block : (k + 1) * block]

    over_columns(n, STEP, body)
    finished = hand_out(me[0], acc, stage, sums_out, sems)

    def finish(i, _):
        pltpu.make_async_copy(act_s.at[i], acts.at[half_cols[i]], asems.at[i]).wait()
        return 0

    lax.fori_loop(0, n, finish, 0)
    for c in finished:
        c.wait()


def backward_kernel(first, last, sizes, slots, parts, *refs):
    refs = list(refs)
    take = lambda n: [refs.pop(0) for _ in range(n)]
    _, half_cols, rows, scales, me = take(5)
    own = take(3)
    (mate,) = take(1)
    others = take(len(sizes))
    g_parts = take(parts)
    (acts_in,) = take(1)
    if not first:
        (sums_in,) = take(1)
    *sums_out, acts = take(3 if last else 2)
    g_s, acc, own_s, mate_s, other_s, act_s, stage, wsems, asems, sems = refs
    n = sum(sizes)
    copies = token_copies(me, g_parts, 1, g_s, sems.at[0])
    for c in copies:
        c.start()
    start_weights(weight_copies(sizes, half_cols, me[1], own, mate, others, own_s, mate_s, other_s, wsems))

    def derivatives(i, away=False):
        here, there = act_s.at[i, pl.ds(1, 2)], acts.at[half_cols[i], pl.ds(1, 2)]
        return pltpu.make_async_copy(here, there, asems.at[i]) if away else pltpu.make_async_copy(there, here, asems.at[i])

    def fetch(i, _):
        derivatives(i).start()
        return 0

    lax.fori_loop(0, n, fetch, 0)
    if first:
        acc[...] = jnp.zeros(acc.shape, F32)
    else:
        sums = pltpu.make_async_copy(sums_in, acc, sems.at[1])
        sums.start()
        sums.wait()
    for c in copies:
        c.wait()
    mine = g_s.shape[1] // 2
    block = g_s.shape[2]

    def body(columns):
        for i in columns:
            wait_weights(own_s, mate_s, other_s, wsems, i)
            derivatives(i).wait()
        kept = []
        for i in columns:
            row, scale = picker(rows, scales, half_cols[i], slots)
            weights = functools.partial(scaled, own_s, mate_s, other_s, scale, i)
            selected = jnp.concatenate([g_s[row(2, k)] for k in range(slots)], axis=1)
            grad_hidden = dot(selected, jnp.concatenate(weights(2), axis=1), 1, 1)
            for m in range(2):
                act = (grad_hidden * act_s[i, 1 + m].astype(F32)).astype(BF16)
                act_s[i, 1 + m] = act
                kept.append((row, m, dot(act[:mine], jnp.concatenate(weights(m), axis=0), 1, 1)))
            derivatives(i, True).start()
        for row, m, back in kept:
            for k in range(slots):
                acc[row(m, k)] += back[:, k * block : (k + 1) * block]

    over_columns(n, STEP, body)
    finished = hand_out(me[0], acc, stage, sums_out, sems)

    def finish(i, _):
        derivatives(i, True).wait()
        return 0

    lax.fori_loop(0, n, finish, 0)
    for c in finished:
        c.wait()


def columns_call(token, backward, first, last, sizes, half_cols, rows, scales, me, own, mate, others, token_parts, sums, acts):
    own_slots, _, block, _ = own[0].shape
    n = sum(sizes)
    nblocks, half_tokens = token_parts[0].shape[0] * token_parts[0].shape[1] // 2, token_parts[0].shape[2]
    tokens = 2 * half_tokens
    args = [token, half_cols, rows, scales, me, *own, mate, *others, *token_parts]
    in_specs = [SMEM] * 5 + [HBM] * 3 + [ANY] * (len(args) - 8)
    aliases = {}
    more = ([acts] if first else [acts, sums]) if backward else ([] if first else [sums, acts])
    for v in more:
        if v is acts or not last:
            aliases[len(args)] = 0 if v is sums else 1 + last
        args.append(v)
        in_specs.append(ANY)
    kernel = backward_kernel if backward else forward_kernel
    sums_out = [jax.ShapeDtypeStruct((nblocks, half_tokens, block), F32)]
    stage = (8, 16, block)
    if last:
        stage = (nblocks, half_tokens // 2, block)
        sums_out = [jax.ShapeDtypeStruct(stage, kind) for kind in (F32, BF16)]
    return pl.pallas_call(
        functools.partial(kernel, first, last, sizes, 4 * own_slots, len(token_parts)),
        in_specs=in_specs,
        out_specs=[ANY] * (len(sums_out) + 1),
        out_shape=[*sums_out, jax.ShapeDtypeStruct((mate.shape[2], 3, tokens, block), BF16)],
        scratch_shapes=[
            pltpu.VMEM((nblocks, tokens, block), BF16),
            pltpu.VMEM((nblocks, half_tokens, block), F32),
            pltpu.VMEM((n, 3, own_slots, block, block), BF16),
            pltpu.VMEM((n, 3, own_slots, block, block), BF16),
            pltpu.VMEM((n, 3, 2 * own_slots, block, block), BF16),
            pltpu.VMEM((n, 3, tokens, block), BF16),
            pltpu.VMEM(stage, BF16),
            pltpu.SemaphoreType.DMA((n,)),
            pltpu.SemaphoreType.DMA((n,)),
            pltpu.SemaphoreType.DMA((2,)),
        ],
        input_output_aliases=aliases,
        compiler_params=PARAMS,
        cost_estimate=estimate(100.0 if backward else 1.0),
        name="backward" if backward else "forward",
    )(*args)


def gradients_kernel(own_slots, slots, count, token, rows, scales, me, *refs):
    parts, refs = refs[:count], refs[count:]
    acts, grad_gate, grad_up, grad_down, grad_mate, x_s, g_s, act_s, out_s, asems, osems, sems = refs
    n = acts.shape[0]
    depth = act_s.shape[0]
    x_copies = token_copies(me, parts, 0, x_s, sems.at[0])
    g_copies = token_copies(me, parts, 1, g_s, sems.at[1])
    for c in x_copies + g_copies:
        c.start()
    grads = (grad_gate, grad_up, grad_down)
    block = x_s.shape[2]
    half = 2 * own_slots

    def fetch(i):
        return pltpu.make_async_copy(acts.at[i], act_s.at[lax.rem(i, depth)], asems.at[lax.rem(i, depth)])

    def stores(i):
        at = lax.rem(i, depth)
        out = [pltpu.make_async_copy(out_s.at[at, m, pl.ds(0, own_slots)], v.at[:, me[1] + i], osems.at[at]) for m, v in enumerate(grads)]
        out.append(pltpu.make_async_copy(out_s.at[at, :, pl.ds(own_slots, own_slots)], grad_mate.at[:, :, i], osems.at[at]))
        return out

    for i in range(depth):
        fetch(i).start()
    for c in x_copies + g_copies:
        c.wait()

    def body(columns):
        for i in columns:
            fetch(i).wait()

            @pl.when(i >= depth)
            def _():
                for c in stores(i - depth):
                    c.wait()

        for i in columns:
            at = lax.rem(i, depth)
            row, scale = picker(rows, scales, i, slots)
            for m, source in ((0, x_s), (1, x_s), (2, g_s)):
                act = act_s[at, (m + 1) % 3]
                selected = jnp.concatenate([source[row(m, k)] for k in range(half)], axis=1)
                out = dot(act, selected, 0, 0)
                for k in range(half):
                    piece = (out[:, k * block : (k + 1) * block] * scale(m, k)).astype(BF16)
                    out_s[at, m, k] = piece if m == 2 else piece.T
        for i in columns:
            for c in stores(i):
                c.start()

            @pl.when(i + depth < n)
            def _():
                fetch(i + depth).start()

    over_columns(n, STEP, body)
    for i in range(n - depth, n):
        for c in stores(i):
            c.wait()


def gradients_call(token, rows, scales, me, parts, acts, own_slots, columns):
    n, _, tokens, block = acts.shape
    nblocks = parts[0].shape[0] * parts[0].shape[1] // 2
    depth = min(4, n)
    grad = jax.ShapeDtypeStruct((own_slots, columns, block, block), BF16)
    return pl.pallas_call(
        functools.partial(gradients_kernel, own_slots, 4 * own_slots, len(parts)),
        in_specs=[SMEM] * 4 + [ANY] * (len(parts) + 1),
        out_specs=[ANY] * 4,
        out_shape=[grad] * 3 + [jax.ShapeDtypeStruct((3, own_slots, n, block, block), BF16)],
        scratch_shapes=[
            pltpu.VMEM((nblocks, tokens, block), BF16),
            pltpu.VMEM((nblocks, tokens, block), BF16),
            pltpu.VMEM((depth, 3, tokens, block), BF16),
            pltpu.VMEM((depth, 3, 2 * own_slots, block, block), BF16),
            pltpu.SemaphoreType.DMA((depth,)),
            pltpu.SemaphoreType.DMA((depth,)),
            pltpu.SemaphoreType.DMA((2,)),
        ],
        compiler_params=PARAMS,
        cost_estimate=estimate(15.0),
        name="gradients",
    )(token, rows, scales, me, *parts, acts)


def hold(v, token):
    return lax.optimization_barrier((v, token))


def copy_kernel(pairs_of, n_in, n_out, *refs):
    me, ins, outs = refs[0], refs[1 : 1 + n_in], refs[1 + n_in : 1 + n_in + n_out]
    stages, sems = refs[1 + n_in + n_out : -1], refs[-1]
    groups = [[pltpu.make_async_copy(a, b, sems.at[j]) for a, b in pairs]
              for j, pairs in enumerate(pairs_of(me, ins, stages))]
    for group in groups:
        for c in group:
            c.start()
    away = [pltpu.make_async_copy(a, b, sems.at[n_out + j]) for j, (a, b) in enumerate(zip(stages, outs))]
    for group, c in zip(groups, away):
        for part in group:
            part.wait()
        c.start()
    for c in away:
        c.wait()


def copies_call(name, pairs_of, me, args, shapes):
    return pl.pallas_call(
        functools.partial(copy_kernel, pairs_of, len(args), len(shapes)),
        in_specs=[SMEM] + [HBM] * len(args),
        out_specs=[ANY] * len(shapes),
        out_shape=[jax.ShapeDtypeStruct(s, BF16) for s in shapes],
        scratch_shapes=[pltpu.VMEM(s, BF16) for s in shapes] + [pltpu.SemaphoreType.DMA((2 * len(shapes),))],
        compiler_params=PARAMS,
        name=name,
    )(me, *args)


def step_kernel(*refs):
    refs[-1][0] = refs[0][0]


def step(token, *arrived, us=0.1):
    return pl.pallas_call(
        step_kernel,
        in_specs=[SMEM] + [ANY] * len(arrived),
        out_specs=SMEM,
        out_shape=jax.ShapeDtypeStruct((1,), jnp.int32),
        cost_estimate=estimate(us),
        name="step",
    )(token, *arrived)


def pieces_kernel(me, keep, more, *pieces):
    run = pieces[0].shape[0]
    for s, piece in enumerate(pieces):
        at = pl.ds(lax.rem(me[4] + s, len(pieces)) * run, run)
        piece[...] = (keep[at] + more[at].astype(F32)).astype(BF16)


def pieces_call(me, keep, more, count):
    nblocks, rest, block = keep.shape
    return pl.pallas_call(
        pieces_kernel,
        in_specs=[SMEM] + [pl.BlockSpec(memory_space=pltpu.VMEM)] * 2,
        out_specs=[pl.BlockSpec(memory_space=pltpu.VMEM)] * count,
        out_shape=[jax.ShapeDtypeStruct((nblocks // count, rest, block), BF16)] * count,
        compiler_params=PARAMS,
        cost_estimate=estimate(0.1 * 3.0),
        name="pieces",
    )(me, keep, more)


def total_kernel(*refs):
    out = refs[-1]
    block = refs[0].shape[2]
    for j in range(refs[0].shape[0]):
        whole = refs[0][j].astype(F32)
        for v in refs[1:-1]:
            whole += v[j].astype(F32)
        out[:, j * block : (j + 1) * block] = whole.astype(BF16)


def total(pieces):
    run, rest, block = pieces[0].shape
    return pl.pallas_call(
        total_kernel,
        out_shape=jax.ShapeDtypeStruct((rest, run * block), BF16),
        cost_estimate=estimate(100.0),
        name="total",
    )(*pieces)


def to_blocks(v, block):
    return jnp.swapaxes(v.reshape(v.shape[0], -1, block), 0, 1)


def local_pairs(tokens, cotangent, gate_values, gate_rows, gate_scale, up_values, up_rows, up_scale,
                down_values, down_cols, down_scale):
    own = (gate_values, up_values, down_values)
    own_slots, columns, block, _ = gate_values.shape
    half = columns // 2
    per_part = half // 2
    core = lax.rem(lax.axis_index("fsdp"), 2)
    part = lax.axis_index("parts")
    first = part * per_part
    swap_core = lambda v: lax.ppermute(v, "fsdp", [(i, i ^ 1) for i in range(4)])
    swap_chip = lambda v: lax.ppermute(v, "fsdp", [(i, i ^ 2) for i in range(4)])
    swap_part = lambda v: lax.ppermute(v, "parts", [(0, 1), (1, 0)])
    me = jnp.stack([core, core * half, (1 - core) * half, first, lax.axis_index("tensor")])

    small = jnp.stack([v.astype(BF16) for v in (gate_rows, up_rows, down_cols, gate_scale, up_scale, down_scale)])
    last = jnp.zeros((block * block,), BF16).at[: small.size].set(small.reshape(-1)).reshape(1, block, block)
    both = jnp.concatenate([to_blocks(tokens, block), to_blocks(cotangent, block), last])
    received = swap_chip(both)

    def mate_pairs(me, ins, outs):
        return [[(w.at[:, pl.ds(me[2], half)], outs[0].at[m]) for m, w in enumerate(ins)]]

    sent = copies_call("mate_blocks", mate_pairs, me, own, [(3, own_slots, half, block, block)])[0]
    mate = swap_core(sent)

    packed = jnp.concatenate([small, received[-1].reshape(-1)[: small.size].reshape(small.shape)], axis=1)
    packed = jnp.stack([packed.reshape(6, 2, own_slots, columns), swap_core(packed).reshape(6, 2, own_slots, columns)], axis=2)
    packed = lax.dynamic_slice_in_dim(packed.reshape(6, -1, columns), core * half, half, axis=2).astype(F32)
    packed = jnp.transpose(packed.reshape(2, 3, -1, half), (0, 3, 1, 2)).reshape(2, -1)
    rows = packed[0].astype(jnp.int32)
    scales = packed[1]

    count = lax.axis_size("tensor")
    shift = lambda v, s: lax.ppermute(v, "tensor", [(i, (i + s) % count) for i in range(count)])

    quotas = (2 * per_part // 5,) * 2
    given = sum(quotas)
    left = per_part - given
    other_first = per_part - first
    spans = [[(first, quotas[0])], [(first + quotas[0], quotas[1])], [(first + given, left), (other_first + given, left)]]
    where = jnp.stack([start for span in spans for start, _ in span]).astype(jnp.int32)

    def chunk_pairs(me, ins, outs):
        out, j = [], 5
        for span, dst in zip(spans, outs):
            pairs, done = [], 0
            for _, size in span:
                to = pl.ds(done, size)
                pairs += [(w.at[:, pl.ds(me[1] + me[j], size)], dst.at[m, pl.ds(0, own_slots), to]) for m, w in enumerate(ins[:3])]
                pairs.append((ins[3].at[:, :, pl.ds(me[j], size)], dst.at[:, pl.ds(own_slots, own_slots), to]))
                done += size
                j += 1
            out.append(pairs)
        return out

    shapes = [(3, 2 * own_slots, sum(size for _, size in span), block, block) for span in spans]
    sends = copies_call("chunk_blocks", chunk_pairs, jnp.concatenate([me, where]), (*own, mate), shapes)
    received, sends = hold(received, sends)
    both = jnp.concatenate([both[:-1], received[:-1]], axis=1)
    pieces = [lax.all_gather(both, "tensor")]
    token = step(jnp.reshape(core, (1,)), both)
    sends, token = hold(sends, token)
    direct = [swap_chip(sends[0]), swap_chip(sends[1])]

    def call(backward, names, sums, acts, token, last=False):
        others, columns = [], []
        for name in names:
            j = int(name[1])
            others.append((direct if name[0] == "a" else relayed)[j])
            for start, size in spans[j]:
                columns.append((start if name[0] == "a" else per_part - first + start - first) + jnp.arange(size, dtype=jnp.int32))
        *sums, acts = columns_call(token, backward, sums is None, last, tuple(v.shape[2] for v in others), jnp.concatenate(columns),
                            rows, scales, me, own, mate, others, parts, sums, acts)
        return sums if last else sums[0], acts

    relayed = []

    def hand_on(j, token):
        held, token = hold(direct[j], token)
        relayed.append(swap_part(held))
        return token

    def send_on(j, token):
        held, token = hold(sends[j], token)
        direct.append(swap_chip(held))
        return token

    token = hand_on(0, step(token, direct[0], us=100.0))
    token = send_on(2, hand_on(1, step(token, direct[1])))
    token = step(token, *pieces, relayed[0], us=100.0)
    pieces, token = hold(pieces, token)
    parts = (*pieces, *(swap_core(v) for v in pieces))
    outs, acts = call(False, ("a0", "b0", "a1"), None, None, token)
    token = step(token, outs, direct[2], relayed[1])
    (keep, send), acts = call(False, ("b1", "a2"), outs, acts, token, True)

    def scattered(keep, send):
        first, *others = pieces_call(me, keep, swap_core(send), count)
        return [first] + [shift(v, s + 1) for s, v in enumerate(others)]

    out_pieces = scattered(keep, send)
    token = step(token, out_pieces[0])
    (keep, send), acts = call(True, ("a0", "b0", "a1", "b1", "a2"), None, acts, token, True)
    in_pieces = scattered(keep, send)
    token = step(token, in_pieces[0])
    *grads, grad_mate = gradients_call(token, rows, scales, me, parts, acts, own_slots, columns)
    layer_out, grad_tokens = total(out_pieces), total(in_pieces)
    grad_mate, grad_tokens = lax.optimization_barrier((swap_core(grad_mate), grad_tokens))
    grads = [lax.dynamic_update_slice(v, grad_mate[m], (0, (1 - core) * half, 0, 0)) for m, v in enumerate(grads)]
    return (layer_out, grad_tokens, *grads)


def scaled_sum(products, factors):
    return jnp.sum(products * factors.astype(jnp.float32)[None, :, :, None], axis=1)


def slot_term(selected, grads, factors):
    return (
        jnp.einsum("tkra,trb->krab", selected, grads, preferred_element_type=jnp.float32)
        * factors[:, :, None, None]
    )


def local_gathered(
    tokens,
    cotangent,
    gate_values,
    gate_rows,
    gate_scale,
    up_values,
    up_rows,
    up_scale,
    down_values,
    down_cols,
    down_scale,
):
    block_size = gate_values.shape[-1]
    token_count = tokens.shape[0]
    tensor_count = lax.axis_size("tensor")
    nblocks = tokens.shape[1] * tensor_count // block_size
    local_blocks = nblocks // tensor_count
    gathered = lax.all_gather(tokens, "tensor", axis=1, tiled=True)
    x_blocks = gathered.reshape(token_count, nblocks, block_size)
    gate_where, up_where, down_where = (
        lax.all_gather(gate_rows, "fsdp", axis=0, tiled=True),
        lax.all_gather(up_rows, "fsdp", axis=0, tiled=True),
        lax.all_gather(down_cols, "fsdp", axis=0, tiled=True),
    )
    gate_blocks, gate_factor, up_blocks, up_factor, down_blocks, down_factor = (
        lax.all_gather(gate_values, "fsdp", axis=0, tiled=True),
        lax.all_gather(gate_scale, "fsdp", axis=0, tiled=True),
        lax.all_gather(up_values, "fsdp", axis=0, tiled=True),
        lax.all_gather(up_scale, "fsdp", axis=0, tiled=True),
        lax.all_gather(down_values, "fsdp", axis=0, tiled=True),
        lax.all_gather(down_scale, "fsdp", axis=0, tiled=True),
    )
    gate_sel = x_blocks[:, gate_where]
    up_sel = x_blocks[:, up_where]
    gate_pre = scaled_sum(
        jnp.einsum("tkra,krab->tkrb", gate_sel, gate_blocks, preferred_element_type=jnp.float32),
        gate_factor,
    )
    up_pre = scaled_sum(
        jnp.einsum("tkra,krab->tkrb", up_sel, up_blocks, preferred_element_type=jnp.float32),
        up_factor,
    )
    sigmoid_gate = jax.nn.sigmoid(gate_pre)
    activated = gate_pre * sigmoid_gate
    hidden = (activated * up_pre).astype(jnp.bfloat16)
    down_float = down_factor.astype(jnp.float32)
    down_scaled = (
        jnp.einsum("trb,krbc->krtc", hidden, down_blocks, preferred_element_type=jnp.float32)
        * down_float[:, :, None, None]
    )
    out_full = (
        jnp.zeros((nblocks, token_count, block_size), jnp.float32).at[down_where].add(down_scaled)
    )
    out_part = lax.psum_scatter(
        out_full.astype(jnp.bfloat16), "tensor", scatter_dimension=0, tiled=True
    ).astype(jnp.float32)
    layer_out = (
        jnp.transpose(out_part, (1, 0, 2))
        .reshape(token_count, local_blocks * block_size)
        .astype(jnp.bfloat16)
    )
    grad_full = lax.all_gather(cotangent, "tensor", axis=1, tiled=True).reshape(
        token_count, nblocks, block_size
    )
    down_sel = grad_full[:, down_where]
    gate_float = gate_factor.astype(jnp.float32)
    up_float = up_factor.astype(jnp.float32)
    grad_hidden = scaled_sum(
        jnp.einsum("tkrc,krbc->tkrb", down_sel, down_blocks, preferred_element_type=jnp.float32),
        down_factor,
    )
    grad_down = lax.psum_scatter(
        (
            jnp.einsum("trb,tkrc->krbc", hidden, down_sel, preferred_element_type=jnp.float32)
            * down_float[:, :, None, None]
        ).astype(jnp.bfloat16),
        "fsdp",
        scatter_dimension=0,
        tiled=True,
    )
    grad_gate_act = (
        grad_hidden * up_pre * sigmoid_gate * (1.0 + gate_pre * (1.0 - sigmoid_gate))
    ).astype(jnp.bfloat16)
    grad_up_act = (grad_hidden * activated).astype(jnp.bfloat16)
    grad_gate = lax.psum_scatter(
        slot_term(gate_sel, grad_gate_act, gate_float).astype(jnp.bfloat16),
        "fsdp",
        scatter_dimension=0,
        tiled=True,
    )
    grad_up = lax.psum_scatter(
        slot_term(up_sel, grad_up_act, up_float).astype(jnp.bfloat16),
        "fsdp",
        scatter_dimension=0,
        tiled=True,
    )
    back_gate = (
        jnp.einsum("trb,krab->krta", grad_gate_act, gate_blocks, preferred_element_type=jnp.float32)
        * gate_float[:, :, None, None]
    )
    back_up = (
        jnp.einsum("trb,krab->krta", grad_up_act, up_blocks, preferred_element_type=jnp.float32)
        * up_float[:, :, None, None]
    )
    in_full = (
        jnp.zeros((nblocks, token_count, block_size), jnp.float32)
        .at[gate_where]
        .add(back_gate)
        .at[up_where]
        .add(back_up)
    )
    in_part = lax.psum_scatter(
        in_full.astype(jnp.bfloat16), "tensor", scatter_dimension=0, tiled=True
    ).astype(jnp.float32)
    grad_tokens = (
        jnp.transpose(in_part, (1, 0, 2))
        .reshape(token_count, local_blocks * block_size)
        .astype(jnp.bfloat16)
    )
    return (layer_out, grad_tokens, grad_gate, grad_up, grad_down)


def local(*args):
    tokens, gate_values = args[0], args[2]
    paired = lax.axis_size("fsdp") == 4 and lax.axis_size("parts") == 2
    if paired and gate_values.shape[1] % 4 == 0 and gate_values.shape[1] >= 16:
        return local_pairs(*args)
    return local_gathered(*args)


def solution(mesh):
    in_specs = (
        P(("parts", "fsdp"), "tensor"),
        P(("parts", "fsdp"), "tensor"),
        P("fsdp", "tensor", None, None),
        P("fsdp", "tensor"),
        P("fsdp", "tensor"),
        P("fsdp", "tensor", None, None),
        P("fsdp", "tensor"),
        P("fsdp", "tensor"),
        P("fsdp", "tensor", None, None),
        P("fsdp", "tensor"),
        P("fsdp", "tensor"),
    )
    out_specs = (
        P(("parts", "fsdp"), "tensor"),
        P(("parts", "fsdp"), "tensor"),
        P(("parts", "fsdp"), "tensor", None, None),
        P(("parts", "fsdp"), "tensor", None, None),
        P(("parts", "fsdp"), "tensor", None, None),
    )
    return jax.shard_map(local, mesh=mesh, in_specs=in_specs, out_specs=out_specs, check_vma=False)
```

```python
import functools

import jax
import jax.numpy as jnp
from jax import lax
from jax.experimental import pallas as pl
from jax.experimental.pallas import tpu as pltpu
from jax.sharding import PartitionSpec as P

F32, BF16 = jnp.float32, jnp.bfloat16
ANY = pl.BlockSpec(memory_space=pl.ANY)
HBM = pl.BlockSpec(memory_space=pltpu.HBM)
SMEM = pl.BlockSpec(memory_space=pltpu.SMEM)
PARAMS = pltpu.CompilerParams(vmem_limit_bytes=50 * 2**20)
STEP = 4


def dot(a, b, ca, cb):
    return lax.dot_general(a, b, (((ca,), (cb,)), ((), ())), preferred_element_type=F32)


def estimate(us):
    return pl.CostEstimate(flops=int(us * 1.1e9), bytes_accessed=int(us * 3.0e6), transcendentals=0)


def over_columns(n, step, body):
    if n // step:

        def run(j, _):
            body([j * step + u for u in range(step)])
            return 0

        lax.fori_loop(0, n // step, run, 0)
    if n % step:
        body([n - n % step + u for u in range(n % step)])


def token_copies(me, parts, which, full, sem):
    out = []
    rest = full.shape[1] // 4
    for core, part in zip((me[0], 1 - me[0]), parts):
        shards, run = part.shape[0], part.shape[1] // 2
        for shard in range(shards):
            for chip in range(2):
                here = part.at[shard, pl.ds(which * run, run), pl.ds(chip * rest, rest), :]
                to = full.at[pl.ds(shard * run, run), pl.ds(pl.multiple_of((2 * chip + core) * rest, rest), rest), :]
                out.append(pltpu.make_async_copy(here, to, sem))
    return out


def weight_copies(sizes, half_cols, base, own, mate, others, own_s, mate_s, other_s, sems):
    out = []
    start = 0
    for size, other in zip(sizes, others):

        def of(i, start=start, other=other):
            h = half_cols[i]
            sem = sems.at[i]
            copies = [pltpu.make_async_copy(w.at[:, base + h], own_s.at[i, m], sem) for m, w in enumerate(own)]
            copies.append(pltpu.make_async_copy(mate.at[:, :, h], mate_s.at[i], sem))
            copies.append(pltpu.make_async_copy(other.at[:, :, i - start], other_s.at[i], sem))
            return copies

        out.append((start, size, of))
        start += size
    return out


def start_weights(copies):
    for start, size, of in copies:

        def go(i, _, of=of):
            for c in of(i):
                c.start()
            return 0

        lax.fori_loop(start, start + size, go, 0)


def scaled(own_s, mate_s, other_s, scale, i, m):
    count = own_s.shape[2]
    blocks = [own_s[i, m, k] for k in range(count)] + [mate_s[i, m, k] for k in range(count)]
    blocks += [other_s[i, m, k] for k in range(2 * count)]
    return [b * scale(m, k).astype(BF16) for k, b in enumerate(blocks)]


def wait_weights(own_s, mate_s, other_s, sems, i):
    for ref in (own_s, mate_s, other_s):
        pltpu.make_async_copy(ref.at[i], ref.at[i], sems.at[i]).wait()


def picker(rows, scales, h, slots):
    return (lambda m, k: rows[h * 3 * slots + m * slots + k]), (lambda m, k: scales[h * 3 * slots + m * slots + k])


def hand_out(core, acc, stage, sums_out, sems):
    if len(sums_out) == 1:
        copies = [pltpu.make_async_copy(acc, sums_out[0], sems.at[1])]
    else:
        rest = acc.shape[1] // 2
        mine, other = (pl.ds(pl.multiple_of(c * rest, rest), rest) for c in (core, 1 - core))
        stage[...] = acc[:, other, :].astype(BF16)
        copies = [pltpu.make_async_copy(stage, sums_out[1], sems.at[0]), pltpu.make_async_copy(acc.at[:, mine, :], sums_out[0], sems.at[1])]
    for c in copies:
        c.start()
    return copies


def forward_kernel(first, last, sizes, slots, parts, *refs):
    refs = list(refs)
    take = lambda n: [refs.pop(0) for _ in range(n)]
    _, half_cols, rows, scales, me = take(5)
    own = take(3)
    (mate,) = take(1)
    others = take(len(sizes))
    x_parts = take(parts)
    if not first:
        sums_in, _ = take(2)
    *sums_out, acts = take(3 if last else 2)
    x_s, acc, own_s, mate_s, other_s, act_s, stage, wsems, asems, sems = refs
    n = sum(sizes)
    copies = token_copies(me, x_parts, 0, x_s, sems.at[0])
    for c in copies:
        c.start()
    start_weights(weight_copies(sizes, half_cols, me[1], own, mate, others, own_s, mate_s, other_s, wsems))
    if first:
        acc[...] = jnp.zeros(acc.shape, F32)
    else:
        sums = pltpu.make_async_copy(sums_in, acc, sems.at[1])
        sums.start()
        sums.wait()
    for c in copies:
        c.wait()
    mine = x_s.shape[1] // 2
    block = x_s.shape[2]

    def body(columns):
        for i in columns:
            wait_weights(own_s, mate_s, other_s, wsems, i)
        kept = []
        for i in columns:
            row, scale = picker(rows, scales, half_cols[i], slots)
            weights = functools.partial(scaled, own_s, mate_s, other_s, scale, i)
            pre = []
            for m in range(2):
                selected = jnp.concatenate([x_s[row(m, k)] for k in range(slots)], axis=1)
                pre.append(dot(selected, jnp.concatenate(weights(m), axis=0), 1, 0))
            gate_pre, up_pre = pre
            s = jax.nn.sigmoid(gate_pre)
            activated = gate_pre * s
            hidden = (activated * up_pre).astype(BF16)
            act_s[i, 0] = hidden
            act_s[i, 1] = (up_pre * s * (1.0 + gate_pre * (1.0 - s))).astype(BF16)
            act_s[i, 2] = activated.astype(BF16)
            pltpu.make_async_copy(act_s.at[i], acts.at[half_cols[i]], asems.at[i]).start()
            kept.append((row, dot(hidden[:mine], jnp.concatenate(weights(2), axis=1), 1, 0)))
        for row, out in kept:
            for k in range(slots):
                acc[row(2, k)] += out[:, k * block : (k + 1) * block]

    over_columns(n, STEP, body)
    finished = hand_out(me[0], acc, stage, sums_out, sems)

    def finish(i, _):
        pltpu.make_async_copy(act_s.at[i], acts.at[half_cols[i]], asems.at[i]).wait()
        return 0

    lax.fori_loop(0, n, finish, 0)
    for c in finished:
        c.wait()


def backward_kernel(first, last, sizes, slots, parts, *refs):
    refs = list(refs)
    take = lambda n: [refs.pop(0) for _ in range(n)]
    _, half_cols, rows, scales, me = take(5)
    own = take(3)
    (mate,) = take(1)
    others = take(len(sizes))
    g_parts = take(parts)
    (acts_in,) = take(1)
    if not first:
        (sums_in,) = take(1)
    *sums_out, acts = take(3 if last else 2)
    g_s, acc, own_s, mate_s, other_s, act_s, stage, wsems, asems, sems = refs
    n = sum(sizes)
    copies = token_copies(me, g_parts, 1, g_s, sems.at[0])
    for c in copies:
        c.start()
    start_weights(weight_copies(sizes, half_cols, me[1], own, mate, others, own_s, mate_s, other_s, wsems))

    def derivatives(i, away=False):
        here, there = act_s.at[i, pl.ds(1, 2)], acts.at[half_cols[i], pl.ds(1, 2)]
        return pltpu.make_async_copy(here, there, asems.at[i]) if away else pltpu.make_async_copy(there, here, asems.at[i])

    def fetch(i, _):
        derivatives(i).start()
        return 0

    lax.fori_loop(0, n, fetch, 0)
    if first:
        acc[...] = jnp.zeros(acc.shape, F32)
    else:
        sums = pltpu.make_async_copy(sums_in, acc, sems.at[1])
        sums.start()
        sums.wait()
    for c in copies:
        c.wait()
    mine = g_s.shape[1] // 2
    block = g_s.shape[2]

    def body(columns):
        for i in columns:
            wait_weights(own_s, mate_s, other_s, wsems, i)
            derivatives(i).wait()
        kept = []
        for i in columns:
            row, scale = picker(rows, scales, half_cols[i], slots)
            weights = functools.partial(scaled, own_s, mate_s, other_s, scale, i)
            selected = jnp.concatenate([g_s[row(2, k)] for k in range(slots)], axis=1)
            grad_hidden = dot(selected, jnp.concatenate(weights(2), axis=1), 1, 1)
            for m in range(2):
                act = (grad_hidden * act_s[i, 1 + m].astype(F32)).astype(BF16)
                act_s[i, 1 + m] = act
                kept.append((row, m, dot(act[:mine], jnp.concatenate(weights(m), axis=0), 1, 1)))
            derivatives(i, True).start()
        for row, m, back in kept:
            for k in range(slots):
                acc[row(m, k)] += back[:, k * block : (k + 1) * block]

    over_columns(n, STEP, body)
    finished = hand_out(me[0], acc, stage, sums_out, sems)

    def finish(i, _):
        derivatives(i, True).wait()
        return 0

    lax.fori_loop(0, n, finish, 0)
    for c in finished:
        c.wait()


def columns_call(token, backward, first, last, sizes, half_cols, rows, scales, me, own, mate, others, token_parts, sums, acts):
    own_slots, _, block, _ = own[0].shape
    n = sum(sizes)
    nblocks, half_tokens = token_parts[0].shape[0] * token_parts[0].shape[1] // 2, token_parts[0].shape[2]
    tokens = 2 * half_tokens
    args = [token, half_cols, rows, scales, me, *own, mate, *others, *token_parts]
    in_specs = [SMEM] * 5 + [HBM] * 3 + [ANY] * (len(args) - 8)
    aliases = {}
    more = ([acts] if first else [acts, sums]) if backward else ([] if first else [sums, acts])
    for v in more:
        if v is acts or not last:
            aliases[len(args)] = 0 if v is sums else 1 + last
        args.append(v)
        in_specs.append(ANY)
    kernel = backward_kernel if backward else forward_kernel
    sums_out = [jax.ShapeDtypeStruct((nblocks, half_tokens, block), F32)]
    stage = (8, 16, block)
    if last:
        stage = (nblocks, half_tokens // 2, block)
        sums_out = [jax.ShapeDtypeStruct(stage, kind) for kind in (F32, BF16)]
    return pl.pallas_call(
        functools.partial(kernel, first, last, sizes, 4 * own_slots, len(token_parts)),
        in_specs=in_specs,
        out_specs=[ANY] * (len(sums_out) + 1),
        out_shape=[*sums_out, jax.ShapeDtypeStruct((mate.shape[2], 3, tokens, block), BF16)],
        scratch_shapes=[
            pltpu.VMEM((nblocks, tokens, block), BF16),
            pltpu.VMEM((nblocks, half_tokens, block), F32),
            pltpu.VMEM((n, 3, own_slots, block, block), BF16),
            pltpu.VMEM((n, 3, own_slots, block, block), BF16),
            pltpu.VMEM((n, 3, 2 * own_slots, block, block), BF16),
            pltpu.VMEM((n, 3, tokens, block), BF16),
            pltpu.VMEM(stage, BF16),
            pltpu.SemaphoreType.DMA((n,)),
            pltpu.SemaphoreType.DMA((n,)),
            pltpu.SemaphoreType.DMA((2,)),
        ],
        input_output_aliases=aliases,
        compiler_params=PARAMS,
        cost_estimate=estimate(100.0 if backward and last else 1.0),
        name="backward" if backward else "forward",
    )(*args)


def gradients_kernel(own_slots, slots, count, token, rows, scales, me, *refs):
    parts, refs = refs[:count], refs[count:]
    acts, grad_gate, grad_up, grad_down, grad_mate, x_s, g_s, act_s, out_s, asems, osems, sems = refs
    n = acts.shape[0]
    depth = act_s.shape[0]
    x_copies = token_copies(me, parts, 0, x_s, sems.at[0])
    g_copies = token_copies(me, parts, 1, g_s, sems.at[1])
    for c in x_copies + g_copies:
        c.start()
    grads = (grad_gate, grad_up, grad_down)
    block = x_s.shape[2]
    half = 2 * own_slots

    def fetch(i):
        return pltpu.make_async_copy(acts.at[i], act_s.at[lax.rem(i, depth)], asems.at[lax.rem(i, depth)])

    def stores(i):
        at = lax.rem(i, depth)
        out = [pltpu.make_async_copy(out_s.at[at, m, pl.ds(0, own_slots)], v.at[:, me[1] + i], osems.at[at]) for m, v in enumerate(grads)]
        out.append(pltpu.make_async_copy(out_s.at[at, :, pl.ds(own_slots, own_slots)], grad_mate.at[:, :, i], osems.at[at]))
        return out

    for i in range(depth):
        fetch(i).start()
    for c in x_copies + g_copies:
        c.wait()

    def body(columns):
        for i in columns:
            fetch(i).wait()

            @pl.when(i >= depth)
            def _():
                for c in stores(i - depth):
                    c.wait()

        for i in columns:
            at = lax.rem(i, depth)
            row, scale = picker(rows, scales, i, slots)
            for m, source in ((0, x_s), (1, x_s), (2, g_s)):
                act = act_s[at, (m + 1) % 3]
                selected = jnp.concatenate([source[row(m, k)] for k in range(half)], axis=1)
                out = dot(act, selected, 0, 0)
                for k in range(half):
                    piece = (out[:, k * block : (k + 1) * block] * scale(m, k)).astype(BF16)
                    out_s[at, m, k] = piece if m == 2 else piece.T
        for i in columns:
            for c in stores(i):
                c.start()

            @pl.when(i + depth < n)
            def _():
                fetch(i + depth).start()

    over_columns(n, 2, body)
    for i in range(n - depth, n):
        for c in stores(i):
            c.wait()


def gradients_call(token, rows, scales, me, parts, acts, own_slots, columns):
    n, _, tokens, block = acts.shape
    nblocks = parts[0].shape[0] * parts[0].shape[1] // 2
    depth = min(8, n)
    grad = jax.ShapeDtypeStruct((own_slots, columns, block, block), BF16)
    return pl.pallas_call(
        functools.partial(gradients_kernel, own_slots, 4 * own_slots, len(parts)),
        in_specs=[SMEM] * 4 + [ANY] * (len(parts) + 1),
        out_specs=[ANY] * 4,
        out_shape=[grad] * 3 + [jax.ShapeDtypeStruct((3, own_slots, n, block, block), BF16)],
        scratch_shapes=[
            pltpu.VMEM((nblocks, tokens, block), BF16),
            pltpu.VMEM((nblocks, tokens, block), BF16),
            pltpu.VMEM((depth, 3, tokens, block), BF16),
            pltpu.VMEM((depth, 3, 2 * own_slots, block, block), BF16),
            pltpu.SemaphoreType.DMA((depth,)),
            pltpu.SemaphoreType.DMA((depth,)),
            pltpu.SemaphoreType.DMA((2,)),
        ],
        compiler_params=PARAMS,
        cost_estimate=estimate(15.0),
        name="gradients",
    )(token, rows, scales, me, *parts, acts)


def hold(v, token):
    return lax.optimization_barrier((v, token))


def copy_kernel(pairs_of, n_in, n_out, *refs):
    me, ins, outs = refs[0], refs[1 : 1 + n_in], refs[1 + n_in : 1 + n_in + n_out]
    stages, sems = refs[1 + n_in + n_out : -1], refs[-1]
    groups = [[pltpu.make_async_copy(a, b, sems.at[j]) for a, b in pairs]
              for j, pairs in enumerate(pairs_of(me, ins, stages))]
    for group in groups:
        for c in group:
            c.start()
    away = [pltpu.make_async_copy(a, b, sems.at[n_out + j]) for j, (a, b) in enumerate(zip(stages, outs))]
    for group, c in zip(groups, away):
        for part in group:
            part.wait()
        c.start()
    for c in away:
        c.wait()


def copies_call(name, pairs_of, me, args, shapes):
    return pl.pallas_call(
        functools.partial(copy_kernel, pairs_of, len(args), len(shapes)),
        in_specs=[SMEM] + [HBM] * len(args),
        out_specs=[ANY] * len(shapes),
        out_shape=[jax.ShapeDtypeStruct(s, BF16) for s in shapes],
        scratch_shapes=[pltpu.VMEM(s, BF16) for s in shapes] + [pltpu.SemaphoreType.DMA((2 * len(shapes),))],
        compiler_params=PARAMS,
        name=name,
    )(me, *args)


def step_kernel(*refs):
    refs[-1][0] = refs[0][0]


def step(token, *arrived, us=0.1):
    return pl.pallas_call(
        step_kernel,
        in_specs=[SMEM] + [ANY] * len(arrived),
        out_specs=SMEM,
        out_shape=jax.ShapeDtypeStruct((1,), jnp.int32),
        cost_estimate=estimate(us),
        name="step",
    )(token, *arrived)


def pieces_kernel(me, keep, more, *pieces):
    run = pieces[0].shape[0]
    for s, piece in enumerate(pieces):
        at = pl.ds(lax.rem(me[4] + s, len(pieces)) * run, run)
        piece[...] = (keep[at] + more[at].astype(F32)).astype(BF16)


def pieces_call(me, keep, more, count):
    nblocks, rest, block = keep.shape
    return pl.pallas_call(
        pieces_kernel,
        in_specs=[SMEM] + [pl.BlockSpec(memory_space=pltpu.VMEM)] * 2,
        out_specs=[pl.BlockSpec(memory_space=pltpu.VMEM)] * count,
        out_shape=[jax.ShapeDtypeStruct((nblocks // count, rest, block), BF16)] * count,
        compiler_params=PARAMS,
        cost_estimate=estimate(0.1 * 3.0),
        name="pieces",
    )(me, keep, more)


def total_kernel(*refs):
    out = refs[-1]
    block = refs[0].shape[2]
    for j in range(refs[0].shape[0]):
        whole = refs[0][j].astype(F32)
        for v in refs[1:-1]:
            whole += v[j].astype(F32)
        out[:, j * block : (j + 1) * block] = whole.astype(BF16)


def total(pieces):
    run, rest, block = pieces[0].shape
    return pl.pallas_call(
        total_kernel,
        out_shape=jax.ShapeDtypeStruct((rest, run * block), BF16),
        cost_estimate=estimate(100.0),
        name="total",
    )(*pieces)


def to_blocks(v, block):
    return jnp.swapaxes(v.reshape(v.shape[0], -1, block), 0, 1)


def local_pairs(tokens, cotangent, gate_values, gate_rows, gate_scale, up_values, up_rows, up_scale,
                down_values, down_cols, down_scale):
    own = (gate_values, up_values, down_values)
    own_slots, columns, block, _ = gate_values.shape
    half = columns // 2
    per_part = half // 2
    core = lax.rem(lax.axis_index("fsdp"), 2)
    part = lax.axis_index("parts")
    first = part * per_part
    swap_core = lambda v: lax.ppermute(v, "fsdp", [(i, i ^ 1) for i in range(4)])
    swap_chip = lambda v: lax.ppermute(v, "fsdp", [(i, i ^ 2) for i in range(4)])
    swap_part = lambda v: lax.ppermute(v, "parts", [(0, 1), (1, 0)])
    me = jnp.stack([core, core * half, (1 - core) * half, first, lax.axis_index("tensor")])

    small = jnp.stack([v.astype(BF16) for v in (gate_rows, up_rows, down_cols, gate_scale, up_scale, down_scale)])
    last = jnp.zeros((block * block,), BF16).at[: small.size].set(small.reshape(-1)).reshape(1, block, block)
    both = jnp.concatenate([to_blocks(tokens, block), to_blocks(cotangent, block), last])
    received = swap_chip(both)

    def mate_pairs(me, ins, outs):
        return [[(w.at[:, pl.ds(me[2], half)], outs[0].at[m]) for m, w in enumerate(ins)]]

    sent = copies_call("mate_blocks", mate_pairs, me, own, [(3, own_slots, half, block, block)])[0]
    mate = swap_core(sent)

    packed = jnp.concatenate([small, received[-1].reshape(-1)[: small.size].reshape(small.shape)], axis=1)
    packed = jnp.stack([packed.reshape(6, 2, own_slots, columns), swap_core(packed).reshape(6, 2, own_slots, columns)], axis=2)
    packed = lax.dynamic_slice_in_dim(packed.reshape(6, -1, columns), core * half, half, axis=2).astype(F32)
    packed = jnp.transpose(packed.reshape(2, 3, -1, half), (0, 3, 1, 2)).reshape(2, -1)
    rows = packed[0].astype(jnp.int32)
    scales = packed[1]

    count = lax.axis_size("tensor")
    shift = lambda v, s: lax.ppermute(v, "tensor", [(i, (i + s) % count) for i in range(count)])

    quotas = (2 * per_part // 5,) * 2
    given = sum(quotas)
    left = per_part - given
    other_first = per_part - first
    spans = [[(first, quotas[0])], [(first + quotas[0], quotas[1])], [(first + given, left), (other_first + given, left)]]
    where = jnp.stack([start for span in spans for start, _ in span]).astype(jnp.int32)

    def chunk_pairs(me, ins, outs):
        out, j = [], 5
        for span, dst in zip(spans, outs):
            pairs, done = [], 0
            for _, size in span:
                to = pl.ds(done, size)
                pairs += [(w.at[:, pl.ds(me[1] + me[j], size)], dst.at[m, pl.ds(0, own_slots), to]) for m, w in enumerate(ins[:3])]
                pairs.append((ins[3].at[:, :, pl.ds(me[j], size)], dst.at[:, pl.ds(own_slots, own_slots), to]))
                done += size
                j += 1
            out.append(pairs)
        return out

    shapes = [(3, 2 * own_slots, sum(size for _, size in span), block, block) for span in spans]
    sends = copies_call("chunk_blocks", chunk_pairs, jnp.concatenate([me, where]), (*own, mate), shapes)
    received, sends = hold(received, sends)
    both = jnp.concatenate([both[:-1], received[:-1]], axis=1)
    pieces = [lax.all_gather(both, "tensor")]
    token = step(jnp.reshape(core, (1,)), both)
    sends, token = hold(sends, token)
    direct = [swap_chip(sends[0]), swap_chip(sends[1])]

    def call(backward, names, sums, acts, token, last=False):
        others, columns = [], []
        for name in names:
            j = int(name[1])
            others.append((direct if name[0] == "a" else relayed)[j])
            for start, size in spans[j]:
                columns.append((start if name[0] == "a" else per_part - first + start - first) + jnp.arange(size, dtype=jnp.int32))
        *sums, acts = columns_call(token, backward, sums is None, last, tuple(v.shape[2] for v in others), jnp.concatenate(columns),
                            rows, scales, me, own, mate, others, parts, sums, acts)
        return sums if last else sums[0], acts

    relayed = []

    def hand_on(j, token):
        held, token = hold(direct[j], token)
        relayed.append(swap_part(held))
        return token

    def send_on(j, token):
        held, token = hold(sends[j], token)
        direct.append(swap_chip(held))
        return token

    token = hand_on(0, step(token, direct[0], us=100.0))
    token = send_on(2, hand_on(1, step(token, direct[1])))
    token = step(token, *pieces, relayed[0], us=100.0)
    pieces, token = hold(pieces, token)
    parts = (*pieces, *(swap_core(v) for v in pieces))
    outs, acts = call(False, ("a0", "b0", "a1"), None, None, token)
    ins, acts = call(True, ("a0", "b0", "a1"), None, acts, token)
    token = step(token, ins, direct[2], relayed[1])
    (keep, send), acts = call(False, ("b1", "a2"), outs, acts, token, True)

    def scattered(keep, send):
        first, *others = pieces_call(me, keep, swap_core(send), count)
        return [first] + [shift(v, s + 1) for s, v in enumerate(others)]

    out_pieces = scattered(keep, send)
    token = step(token, out_pieces[0])
    (keep, send), acts = call(True, ("b1", "a2"), ins, acts, token, True)
    in_pieces = scattered(keep, send)
    token = step(token, in_pieces[0])
    *grads, grad_mate = gradients_call(token, rows, scales, me, parts, acts, own_slots, columns)
    layer_out, grad_tokens = total(out_pieces), total(in_pieces)
    grad_mate, grad_tokens = lax.optimization_barrier((swap_core(grad_mate), grad_tokens))
    grads = [lax.dynamic_update_slice(v, grad_mate[m], (0, (1 - core) * half, 0, 0)) for m, v in enumerate(grads)]
    return (layer_out, grad_tokens, *grads)


def scaled_sum(products, factors):
    return jnp.sum(products * factors.astype(jnp.float32)[None, :, :, None], axis=1)


def slot_term(selected, grads, factors):
    return (
        jnp.einsum("tkra,trb->krab", selected, grads, preferred_element_type=jnp.float32)
        * factors[:, :, None, None]
    )


def local_gathered(
    tokens,
    cotangent,
    gate_values,
    gate_rows,
    gate_scale,
    up_values,
    up_rows,
    up_scale,
    down_values,
    down_cols,
    down_scale,
):
    block_size = gate_values.shape[-1]
    token_count = tokens.shape[0]
    tensor_count = lax.axis_size("tensor")
    nblocks = tokens.shape[1] * tensor_count // block_size
    local_blocks = nblocks // tensor_count
    gathered = lax.all_gather(tokens, "tensor", axis=1, tiled=True)
    x_blocks = gathered.reshape(token_count, nblocks, block_size)
    gate_where, up_where, down_where = (
        lax.all_gather(gate_rows, "fsdp", axis=0, tiled=True),
        lax.all_gather(up_rows, "fsdp", axis=0, tiled=True),
        lax.all_gather(down_cols, "fsdp", axis=0, tiled=True),
    )
    gate_blocks, gate_factor, up_blocks, up_factor, down_blocks, down_factor = (
        lax.all_gather(gate_values, "fsdp", axis=0, tiled=True),
        lax.all_gather(gate_scale, "fsdp", axis=0, tiled=True),
        lax.all_gather(up_values, "fsdp", axis=0, tiled=True),
        lax.all_gather(up_scale, "fsdp", axis=0, tiled=True),
        lax.all_gather(down_values, "fsdp", axis=0, tiled=True),
        lax.all_gather(down_scale, "fsdp", axis=0, tiled=True),
    )
    gate_sel = x_blocks[:, gate_where]
    up_sel = x_blocks[:, up_where]
    gate_pre = scaled_sum(
        jnp.einsum("tkra,krab->tkrb", gate_sel, gate_blocks, preferred_element_type=jnp.float32),
        gate_factor,
    )
    up_pre = scaled_sum(
        jnp.einsum("tkra,krab->tkrb", up_sel, up_blocks, preferred_element_type=jnp.float32),
        up_factor,
    )
    sigmoid_gate = jax.nn.sigmoid(gate_pre)
    activated = gate_pre * sigmoid_gate
    hidden = (activated * up_pre).astype(jnp.bfloat16)
    down_float = down_factor.astype(jnp.float32)
    down_scaled = (
        jnp.einsum("trb,krbc->krtc", hidden, down_blocks, preferred_element_type=jnp.float32)
        * down_float[:, :, None, None]
    )
    out_full = (
        jnp.zeros((nblocks, token_count, block_size), jnp.float32).at[down_where].add(down_scaled)
    )
    out_part = lax.psum_scatter(
        out_full.astype(jnp.bfloat16), "tensor", scatter_dimension=0, tiled=True
    ).astype(jnp.float32)
    layer_out = (
        jnp.transpose(out_part, (1, 0, 2))
        .reshape(token_count, local_blocks * block_size)
        .astype(jnp.bfloat16)
    )
    grad_full = lax.all_gather(cotangent, "tensor", axis=1, tiled=True).reshape(
        token_count, nblocks, block_size
    )
    down_sel = grad_full[:, down_where]
    gate_float = gate_factor.astype(jnp.float32)
    up_float = up_factor.astype(jnp.float32)
    grad_hidden = scaled_sum(
        jnp.einsum("tkrc,krbc->tkrb", down_sel, down_blocks, preferred_element_type=jnp.float32),
        down_factor,
    )
    grad_down = lax.psum_scatter(
        (
            jnp.einsum("trb,tkrc->krbc", hidden, down_sel, preferred_element_type=jnp.float32)
            * down_float[:, :, None, None]
        ).astype(jnp.bfloat16),
        "fsdp",
        scatter_dimension=0,
        tiled=True,
    )
    grad_gate_act = (
        grad_hidden * up_pre * sigmoid_gate * (1.0 + gate_pre * (1.0 - sigmoid_gate))
    ).astype(jnp.bfloat16)
    grad_up_act = (grad_hidden * activated).astype(jnp.bfloat16)
    grad_gate = lax.psum_scatter(
        slot_term(gate_sel, grad_gate_act, gate_float).astype(jnp.bfloat16),
        "fsdp",
        scatter_dimension=0,
        tiled=True,
    )
    grad_up = lax.psum_scatter(
        slot_term(up_sel, grad_up_act, up_float).astype(jnp.bfloat16),
        "fsdp",
        scatter_dimension=0,
        tiled=True,
    )
    back_gate = (
        jnp.einsum("trb,krab->krta", grad_gate_act, gate_blocks, preferred_element_type=jnp.float32)
        * gate_float[:, :, None, None]
    )
    back_up = (
        jnp.einsum("trb,krab->krta", grad_up_act, up_blocks, preferred_element_type=jnp.float32)
        * up_float[:, :, None, None]
    )
    in_full = (
        jnp.zeros((nblocks, token_count, block_size), jnp.float32)
        .at[gate_where]
        .add(back_gate)
        .at[up_where]
        .add(back_up)
    )
    in_part = lax.psum_scatter(
        in_full.astype(jnp.bfloat16), "tensor", scatter_dimension=0, tiled=True
    ).astype(jnp.float32)
    grad_tokens = (
        jnp.transpose(in_part, (1, 0, 2))
        .reshape(token_count, local_blocks * block_size)
        .astype(jnp.bfloat16)
    )
    return (layer_out, grad_tokens, grad_gate, grad_up, grad_down)


def local(*args):
    tokens, gate_values = args[0], args[2]
    paired = lax.axis_size("fsdp") == 4 and lax.axis_size("parts") == 2
    if paired and gate_values.shape[1] % 4 == 0 and gate_values.shape[1] >= 16:
        return local_pairs(*args)
    return local_gathered(*args)


def solution(mesh):
    in_specs = (
        P(("parts", "fsdp"), "tensor"),
        P(("parts", "fsdp"), "tensor"),
        P("fsdp", "tensor", None, None),
        P("fsdp", "tensor"),
        P("fsdp", "tensor"),
        P("fsdp", "tensor", None, None),
        P("fsdp", "tensor"),
        P("fsdp", "tensor"),
        P("fsdp", "tensor", None, None),
        P("fsdp", "tensor"),
        P("fsdp", "tensor"),
    )
    out_specs = (
        P(("parts", "fsdp"), "tensor"),
        P(("parts", "fsdp"), "tensor"),
        P(("parts", "fsdp"), "tensor", None, None),
        P(("parts", "fsdp"), "tensor", None, None),
        P(("parts", "fsdp"), "tensor", None, None),
    )
    return jax.shard_map(local, mesh=mesh, in_specs=in_specs, out_specs=out_specs, check_vma=False)
```

```python
import functools

import jax
import jax.numpy as jnp
from jax import lax
from jax.experimental import pallas as pl
from jax.experimental.pallas import tpu as pltpu
from jax.sharding import PartitionSpec as P

F32, BF16 = jnp.float32, jnp.bfloat16
ANY = pl.BlockSpec(memory_space=pl.ANY)
HBM = pl.BlockSpec(memory_space=pltpu.HBM)
SMEM = pl.BlockSpec(memory_space=pltpu.SMEM)
PARAMS = pltpu.CompilerParams(vmem_limit_bytes=50 * 2**20)
STEP = 4


def dot(a, b, ca, cb):
    return lax.dot_general(a, b, (((ca,), (cb,)), ((), ())), preferred_element_type=F32)


def estimate(us):
    return pl.CostEstimate(flops=int(us * 1.1e9), bytes_accessed=int(us * 3.0e6), transcendentals=0)


def over_columns(n, step, body):
    if n // step:

        def run(j, _):
            body([j * step + u for u in range(step)])
            return 0

        lax.fori_loop(0, n // step, run, 0)
    if n % step:
        body([n - n % step + u for u in range(n % step)])


def token_copies(me, parts, which, full, sem):
    out = []
    rest = full.shape[1] // 4
    for core, part in zip((me[0], 1 - me[0]), parts):
        shards, run = part.shape[0], part.shape[1] // 2
        for shard in range(shards):
            for chip in range(2):
                here = part.at[shard, pl.ds(which * run, run), pl.ds(chip * rest, rest), :]
                to = full.at[pl.ds(shard * run, run), pl.ds(pl.multiple_of((2 * chip + core) * rest, rest), rest), :]
                out.append(pltpu.make_async_copy(here, to, sem))
    return out


def weight_copies(sizes, half_cols, base, own, mate, others, own_s, mate_s, other_s, sems):
    out = []
    start = 0
    for size, other in zip(sizes, others):

        def of(i, start=start, other=other):
            h = half_cols[i]
            sem = sems.at[i]
            copies = [pltpu.make_async_copy(w.at[:, base + h], own_s.at[i, m], sem) for m, w in enumerate(own)]
            copies.append(pltpu.make_async_copy(mate.at[:, :, h], mate_s.at[i], sem))
            copies.append(pltpu.make_async_copy(other.at[:, :, i - start], other_s.at[i], sem))
            return copies

        out.append((start, size, of))
        start += size
    return out


def start_weights(copies, more=None):
    for start, size, of in copies:

        def go(i, _, of=of):
            for c in of(i) + ([more(i)] if more else []):
                c.start()
            return 0

        lax.fori_loop(start, start + size, go, 0)


def scaled(own_s, mate_s, other_s, scale, i, m):
    count = own_s.shape[2]
    blocks = [own_s[i, m, k] for k in range(count)] + [mate_s[i, m, k] for k in range(count)]
    blocks += [other_s[i, m, k] for k in range(2 * count)]
    return [b * scale(m, k).astype(BF16) for k, b in enumerate(blocks)]


def wait_weights(own_s, mate_s, other_s, sems, i):
    for ref in (own_s, mate_s, other_s):
        pltpu.make_async_copy(ref.at[i], ref.at[i], sems.at[i]).wait()


def picker(rows, scales, h, slots):
    return (lambda m, k: rows[h * 3 * slots + m * slots + k]), (lambda m, k: scales[h * 3 * slots + m * slots + k])


def hand_out(core, acc, stage, sums_out, sems):
    if len(sums_out) == 1:
        copies = [pltpu.make_async_copy(acc, sums_out[0], sems.at[1])]
    else:
        rest = acc.shape[1] // 2
        mine, other = (pl.ds(pl.multiple_of(c * rest, rest), rest) for c in (core, 1 - core))
        stage[...] = acc[:, other, :].astype(BF16)
        copies = [pltpu.make_async_copy(stage, sums_out[1], sems.at[0]), pltpu.make_async_copy(acc.at[:, mine, :], sums_out[0], sems.at[1])]
    for c in copies:
        c.start()
    return copies


def forward_kernel(first, last, sizes, slots, parts, *refs):
    refs = list(refs)
    take = lambda n: [refs.pop(0) for _ in range(n)]
    _, half_cols, rows, scales, me = take(5)
    own = take(3)
    (mate,) = take(1)
    others = take(len(sizes))
    x_parts = take(parts)
    if not first:
        sums_in, _ = take(2)
    *sums_out, acts = take(3 if last else 2)
    x_s, acc, own_s, mate_s, other_s, act_s, stage, wsems, asems, sems = refs
    n = sum(sizes)
    copies = token_copies(me, x_parts, 0, x_s, sems.at[0])
    for c in copies:
        c.start()
    if not first:
        sums = pltpu.make_async_copy(sums_in, acc, sems.at[1])
        sums.start()
    start_weights(weight_copies(sizes, half_cols, me[1], own, mate, others, own_s, mate_s, other_s, wsems))
    if first:
        acc[...] = jnp.zeros(acc.shape, F32)
    else:
        sums.wait()
    for c in copies:
        c.wait()
    mine = x_s.shape[1] // 2
    block = x_s.shape[2]

    def body(columns):
        for i in columns:
            wait_weights(own_s, mate_s, other_s, wsems, i)
        kept = []
        for i in columns:
            row, scale = picker(rows, scales, half_cols[i], slots)
            weights = functools.partial(scaled, own_s, mate_s, other_s, scale, i)
            pre = []
            for m in range(2):
                selected = jnp.concatenate([x_s[row(m, k)] for k in range(slots)], axis=1)
                pre.append(dot(selected, jnp.concatenate(weights(m), axis=0), 1, 0))
            gate_pre, up_pre = pre
            s = jax.nn.sigmoid(gate_pre)
            activated = gate_pre * s
            hidden = (activated * up_pre).astype(BF16)
            act_s[i, 0] = hidden
            act_s[i, 1] = (up_pre * s * (1.0 + gate_pre * (1.0 - s))).astype(BF16)
            act_s[i, 2] = activated.astype(BF16)
            pltpu.make_async_copy(act_s.at[i], acts.at[half_cols[i]], asems.at[i]).start()
            kept.append((row, dot(hidden[:mine], jnp.concatenate(weights(2), axis=1), 1, 0)))
        for row, out in kept:
            for k in range(slots):
                acc[row(2, k)] += out[:, k * block : (k + 1) * block]

    over_columns(n, STEP, body)
    finished = hand_out(me[0], acc, stage, sums_out, sems)

    def finish(i, _):
        pltpu.make_async_copy(act_s.at[i], acts.at[half_cols[i]], asems.at[i]).wait()
        return 0

    lax.fori_loop(0, n, finish, 0)
    for c in finished:
        c.wait()


def backward_kernel(first, last, sizes, slots, parts, *refs):
    refs = list(refs)
    take = lambda n: [refs.pop(0) for _ in range(n)]
    _, half_cols, rows, scales, me = take(5)
    own = take(3)
    (mate,) = take(1)
    others = take(len(sizes))
    g_parts = take(parts)
    (acts_in,) = take(1)
    if not first:
        (sums_in,) = take(1)
    *sums_out, acts = take(3 if last else 2)
    g_s, acc, own_s, mate_s, other_s, act_s, stage, wsems, asems, sems = refs
    n = sum(sizes)
    copies = token_copies(me, g_parts, 1, g_s, sems.at[0])
    for c in copies:
        c.start()

    def derivatives(i, away=False):
        here, there = act_s.at[i, pl.ds(1, 2)], acts.at[half_cols[i], pl.ds(1, 2)]
        return pltpu.make_async_copy(here, there, asems.at[i]) if away else pltpu.make_async_copy(there, here, asems.at[i])

    if not first:
        sums = pltpu.make_async_copy(sums_in, acc, sems.at[1])
        sums.start()
    weights = weight_copies(sizes, half_cols, me[1], own, mate, others, own_s, mate_s, other_s, wsems)
    start_weights(weights, derivatives)
    if first:
        acc[...] = jnp.zeros(acc.shape, F32)
    else:
        sums.wait()
    for c in copies:
        c.wait()
    mine = g_s.shape[1] // 2
    block = g_s.shape[2]

    def body(columns):
        for i in columns:
            wait_weights(own_s, mate_s, other_s, wsems, i)
            derivatives(i).wait()
        kept = []
        for i in columns:
            row, scale = picker(rows, scales, half_cols[i], slots)
            weights = functools.partial(scaled, own_s, mate_s, other_s, scale, i)
            selected = jnp.concatenate([g_s[row(2, k)] for k in range(slots)], axis=1)
            grad_hidden = dot(selected, jnp.concatenate(weights(2), axis=1), 1, 1)
            for m in range(2):
                act = (grad_hidden * act_s[i, 1 + m].astype(F32)).astype(BF16)
                act_s[i, 1 + m] = act
                kept.append((row, m, dot(act[:mine], jnp.concatenate(weights(m), axis=0), 1, 1)))
            derivatives(i, True).start()
        for row, m, back in kept:
            for k in range(slots):
                acc[row(m, k)] += back[:, k * block : (k + 1) * block]

    over_columns(n, STEP, body)
    finished = hand_out(me[0], acc, stage, sums_out, sems)

    def finish(i, _):
        derivatives(i, True).wait()
        return 0

    lax.fori_loop(0, n, finish, 0)
    for c in finished:
        c.wait()


def columns_call(token, backward, first, last, sizes, half_cols, rows, scales, me, own, mate, others, token_parts, sums, acts):
    own_slots, _, block, _ = own[0].shape
    n = sum(sizes)
    nblocks, half_tokens = token_parts[0].shape[0] * token_parts[0].shape[1] // 2, token_parts[0].shape[2]
    tokens = 2 * half_tokens
    args = [token, half_cols, rows, scales, me, *own, mate, *others, *token_parts]
    in_specs = [SMEM] * 5 + [HBM] * 3 + [ANY] * (len(args) - 8)
    aliases = {}
    more = ([acts] if first else [acts, sums]) if backward else ([] if first else [sums, acts])
    for v in more:
        if v is acts or not last:
            aliases[len(args)] = 0 if v is sums else 1 + last
        args.append(v)
        in_specs.append(ANY)
    kernel = backward_kernel if backward else forward_kernel
    sums_out = [jax.ShapeDtypeStruct((nblocks, half_tokens, block), F32)]
    stage = (8, 16, block)
    if last:
        stage = (nblocks, half_tokens // 2, block)
        sums_out = [jax.ShapeDtypeStruct(stage, kind) for kind in (F32, BF16)]
    return pl.pallas_call(
        functools.partial(kernel, first, last, sizes, 4 * own_slots, len(token_parts)),
        in_specs=in_specs,
        out_specs=[ANY] * (len(sums_out) + 1),
        out_shape=[*sums_out, jax.ShapeDtypeStruct((mate.shape[2], 3, tokens, block), BF16)],
        scratch_shapes=[
            pltpu.VMEM((nblocks, tokens, block), BF16),
            pltpu.VMEM((nblocks, half_tokens, block), F32),
            pltpu.VMEM((n, 3, own_slots, block, block), BF16),
            pltpu.VMEM((n, 3, own_slots, block, block), BF16),
            pltpu.VMEM((n, 3, 2 * own_slots, block, block), BF16),
            pltpu.VMEM((n, 3, tokens, block), BF16),
            pltpu.VMEM(stage, BF16),
            pltpu.SemaphoreType.DMA((n,)),
            pltpu.SemaphoreType.DMA((n,)),
            pltpu.SemaphoreType.DMA((2,)),
        ],
        input_output_aliases=aliases,
        compiler_params=PARAMS,
        cost_estimate=estimate(100.0 if backward and last else 1.0),
        name="backward" if backward else "forward",
    )(*args)


def gradients_kernel(own_slots, slots, count, token, rows, scales, me, *refs):
    parts, refs = refs[:count], refs[count:]
    acts, grad_gate, grad_up, grad_down, grad_mate, x_s, g_s, act_s, out_s, asems, osems, sems = refs
    n = acts.shape[0]
    depth = act_s.shape[0]
    x_copies = token_copies(me, parts, 0, x_s, sems.at[0])
    g_copies = token_copies(me, parts, 1, g_s, sems.at[1])
    for c in x_copies + g_copies:
        c.start()
    grads = (grad_gate, grad_up, grad_down)
    block = x_s.shape[2]
    half = 2 * own_slots

    def fetch(i):
        return pltpu.make_async_copy(acts.at[i], act_s.at[lax.rem(i, depth)], asems.at[lax.rem(i, depth)])

    def stores(i):
        at = lax.rem(i, depth)
        out = [pltpu.make_async_copy(out_s.at[at, m, pl.ds(0, own_slots)], v.at[:, me[1] + i], osems.at[at]) for m, v in enumerate(grads)]
        out.append(pltpu.make_async_copy(out_s.at[at, :, pl.ds(own_slots, own_slots)], grad_mate.at[:, :, i], osems.at[at]))
        return out

    for i in range(depth):
        fetch(i).start()
    for c in x_copies + g_copies:
        c.wait()

    def body(columns):
        for i in columns:
            fetch(i).wait()

            @pl.when(i >= depth)
            def _():
                for c in stores(i - depth):
                    c.wait()

        for i in columns:
            at = lax.rem(i, depth)
            row, scale = picker(rows, scales, i, slots)
            for m, source in ((0, x_s), (1, x_s), (2, g_s)):
                act = act_s[at, (m + 1) % 3]
                selected = jnp.concatenate([source[row(m, k)] for k in range(half)], axis=1)
                out = dot(act, selected, 0, 0)
                for k in range(half):
                    piece = (out[:, k * block : (k + 1) * block] * scale(m, k)).astype(BF16)
                    out_s[at, m, k] = piece if m == 2 else piece.T
        for i in columns:
            for c in stores(i):
                c.start()

            @pl.when(i + depth < n)
            def _():
                fetch(i + depth).start()

    over_columns(n, 2, body)
    for i in range(n - depth, n):
        for c in stores(i):
            c.wait()


def gradients_call(token, rows, scales, me, parts, acts, own_slots, columns):
    n, _, tokens, block = acts.shape
    nblocks = parts[0].shape[0] * parts[0].shape[1] // 2
    depth = min(8, n)
    grad = jax.ShapeDtypeStruct((own_slots, columns, block, block), BF16)
    return pl.pallas_call(
        functools.partial(gradients_kernel, own_slots, 4 * own_slots, len(parts)),
        in_specs=[SMEM] * 4 + [ANY] * (len(parts) + 1),
        out_specs=[ANY] * 4,
        out_shape=[grad] * 3 + [jax.ShapeDtypeStruct((3, own_slots, n, block, block), BF16)],
        scratch_shapes=[
            pltpu.VMEM((nblocks, tokens, block), BF16),
            pltpu.VMEM((nblocks, tokens, block), BF16),
            pltpu.VMEM((depth, 3, tokens, block), BF16),
            pltpu.VMEM((depth, 3, 2 * own_slots, block, block), BF16),
            pltpu.SemaphoreType.DMA((depth,)),
            pltpu.SemaphoreType.DMA((depth,)),
            pltpu.SemaphoreType.DMA((2,)),
        ],
        compiler_params=PARAMS,
        cost_estimate=estimate(15.0),
        name="gradients",
    )(token, rows, scales, me, *parts, acts)


def hold(v, token):
    return lax.optimization_barrier((v, token))


def copy_kernel(pairs_of, n_in, n_out, *refs):
    me, ins, outs = refs[0], refs[1 : 1 + n_in], refs[1 + n_in : 1 + n_in + n_out]
    stages, sems = refs[1 + n_in + n_out : -1], refs[-1]
    groups = [[pltpu.make_async_copy(a, b, sems.at[j]) for a, b in pairs]
              for j, pairs in enumerate(pairs_of(me, ins, stages))]
    for group in groups:
        for c in group:
            c.start()
    away = [pltpu.make_async_copy(a, b, sems.at[n_out + j]) for j, (a, b) in enumerate(zip(stages, outs))]
    for group, c in zip(groups, away):
        for part in group:
            part.wait()
        c.start()
    for c in away:
        c.wait()


def copies_call(name, pairs_of, me, args, shapes):
    return pl.pallas_call(
        functools.partial(copy_kernel, pairs_of, len(args), len(shapes)),
        in_specs=[SMEM] + [HBM] * len(args),
        out_specs=[ANY] * len(shapes),
        out_shape=[jax.ShapeDtypeStruct(s, BF16) for s in shapes],
        scratch_shapes=[pltpu.VMEM(s, BF16) for s in shapes] + [pltpu.SemaphoreType.DMA((2 * len(shapes),))],
        compiler_params=PARAMS,
        name=name,
    )(me, *args)


def step_kernel(*refs):
    refs[-1][0] = refs[0][0]


def step(token, *arrived, us=0.1):
    return pl.pallas_call(
        step_kernel,
        in_specs=[SMEM] + [ANY] * len(arrived),
        out_specs=SMEM,
        out_shape=jax.ShapeDtypeStruct((1,), jnp.int32),
        cost_estimate=estimate(us),
        name="step",
    )(token, *arrived)


def pieces_kernel(me, keep, more, *pieces):
    run = pieces[0].shape[0]
    for s, piece in enumerate(pieces):
        at = pl.ds(lax.rem(me[4] + s, len(pieces)) * run, run)
        piece[...] = (keep[at] + more[at].astype(F32)).astype(BF16)


def pieces_call(me, keep, more, count):
    nblocks, rest, block = keep.shape
    return pl.pallas_call(
        pieces_kernel,
        in_specs=[SMEM] + [pl.BlockSpec(memory_space=pltpu.VMEM)] * 2,
        out_specs=[pl.BlockSpec(memory_space=pltpu.VMEM)] * count,
        out_shape=[jax.ShapeDtypeStruct((nblocks // count, rest, block), BF16)] * count,
        compiler_params=PARAMS,
        cost_estimate=estimate(0.1 * 3.0),
        name="pieces",
    )(me, keep, more)


def total_kernel(*refs):
    out = refs[-1]
    block = refs[0].shape[2]
    for j in range(refs[0].shape[0]):
        whole = refs[0][j].astype(F32)
        for v in refs[1:-1]:
            whole += v[j].astype(F32)
        out[:, j * block : (j + 1) * block] = whole.astype(BF16)


def total(pieces):
    run, rest, block = pieces[0].shape
    return pl.pallas_call(
        total_kernel,
        out_shape=jax.ShapeDtypeStruct((rest, run * block), BF16),
        cost_estimate=estimate(100.0),
        name="total",
    )(*pieces)


def to_blocks(v, block):
    return jnp.swapaxes(v.reshape(v.shape[0], -1, block), 0, 1)


def local_pairs(tokens, cotangent, gate_values, gate_rows, gate_scale, up_values, up_rows, up_scale,
                down_values, down_cols, down_scale):
    own = (gate_values, up_values, down_values)
    own_slots, columns, block, _ = gate_values.shape
    half = columns // 2
    per_part = half // 2
    core = lax.rem(lax.axis_index("fsdp"), 2)
    part = lax.axis_index("parts")
    first = part * per_part
    swap_core = lambda v: lax.ppermute(v, "fsdp", [(i, i ^ 1) for i in range(4)])
    swap_chip = lambda v: lax.ppermute(v, "fsdp", [(i, i ^ 2) for i in range(4)])
    swap_part = lambda v: lax.ppermute(v, "parts", [(0, 1), (1, 0)])
    me = jnp.stack([core, core * half, (1 - core) * half, first, lax.axis_index("tensor")])

    small = jnp.stack([v.astype(BF16) for v in (gate_rows, up_rows, down_cols, gate_scale, up_scale, down_scale)])
    last = jnp.zeros((block * block,), BF16).at[: small.size].set(small.reshape(-1)).reshape(1, block, block)
    both = jnp.concatenate([to_blocks(tokens, block), to_blocks(cotangent, block), last])
    received = swap_chip(both)

    def mate_pairs(me, ins, outs):
        return [[(w.at[:, pl.ds(me[2], half)], outs[0].at[m]) for m, w in enumerate(ins)]]

    sent = copies_call("mate_blocks", mate_pairs, me, own, [(3, own_slots, half, block, block)])[0]
    mate = swap_core(sent)

    packed = jnp.concatenate([small, received[-1].reshape(-1)[: small.size].reshape(small.shape)], axis=1)
    packed = jnp.stack([packed.reshape(6, 2, own_slots, columns), swap_core(packed).reshape(6, 2, own_slots, columns)], axis=2)
    packed = lax.dynamic_slice_in_dim(packed.reshape(6, -1, columns), core * half, half, axis=2).astype(F32)
    packed = jnp.transpose(packed.reshape(2, 3, -1, half), (0, 3, 1, 2)).reshape(2, -1)
    rows = packed[0].astype(jnp.int32)
    scales = packed[1]

    count = lax.axis_size("tensor")
    shift = lambda v, s: lax.ppermute(v, "tensor", [(i, (i + s) % count) for i in range(count)])

    quotas = (2 * per_part // 5,) * 2
    given = sum(quotas)
    left = per_part - given
    other_first = per_part - first
    spans = [[(first, quotas[0])], [(first + quotas[0], quotas[1])], [(first + given, left), (other_first + given, left)]]
    where = jnp.stack([start for span in spans for start, _ in span]).astype(jnp.int32)

    def chunk_pairs(me, ins, outs):
        out, j = [], 5
        for span, dst in zip(spans, outs):
            pairs, done = [], 0
            for _, size in span:
                to = pl.ds(done, size)
                pairs += [(w.at[:, pl.ds(me[1] + me[j], size)], dst.at[m, pl.ds(0, own_slots), to]) for m, w in enumerate(ins[:3])]
                pairs.append((ins[3].at[:, :, pl.ds(me[j], size)], dst.at[:, pl.ds(own_slots, own_slots), to]))
                done += size
                j += 1
            out.append(pairs)
        return out

    shapes = [(3, 2 * own_slots, sum(size for _, size in span), block, block) for span in spans]
    sends = copies_call("chunk_blocks", chunk_pairs, jnp.concatenate([me, where]), (*own, mate), shapes)
    received, sends = hold(received, sends)
    both = jnp.concatenate([both[:-1], received[:-1]], axis=1)
    pieces = [lax.all_gather(both, "tensor")]
    token = step(jnp.reshape(core, (1,)), both)
    sends, token = hold(sends, token)
    direct = [swap_chip(sends[0]), swap_chip(sends[1])]

    def call(backward, names, sums, acts, token, last=False):
        others, columns = [], []
        for name in names:
            j = int(name[1])
            others.append((direct if name[0] == "a" else relayed)[j])
            for start, size in spans[j]:
                columns.append((start if name[0] == "a" else per_part - first + start - first) + jnp.arange(size, dtype=jnp.int32))
        *sums, acts = columns_call(token, backward, sums is None, last, tuple(v.shape[2] for v in others), jnp.concatenate(columns),
                            rows, scales, me, own, mate, others, parts, sums, acts)
        return sums if last else sums[0], acts

    relayed = []

    def hand_on(j, token):
        held, token = hold(direct[j], token)
        relayed.append(swap_part(held))
        return token

    def send_on(j, token):
        held, token = hold(sends[j], token)
        direct.append(swap_chip(held))
        return token

    token = hand_on(0, step(token, direct[0], us=100.0))
    token = send_on(2, hand_on(1, step(token, direct[1])))
    token = step(token, *pieces, relayed[0], us=100.0)
    pieces, token = hold(pieces, token)
    parts = (*pieces, *(swap_core(v) for v in pieces))
    outs, acts = call(False, ("a0", "b0", "a1"), None, None, token)
    ins, acts = call(True, ("a0", "b0", "a1"), None, acts, token)
    token = step(token, ins, direct[2], relayed[1])
    (keep, send), acts = call(False, ("b1", "a2"), outs, acts, token, True)

    def scattered(keep, send):
        first, *others = pieces_call(me, keep, swap_core(send), count)
        return [first] + [shift(v, s + 1) for s, v in enumerate(others)]

    out_pieces = scattered(keep, send)
    token = step(token, out_pieces[0])
    (keep, send), acts = call(True, ("b1", "a2"), ins, acts, token, True)
    in_pieces = scattered(keep, send)
    token = step(token, in_pieces[0])
    *grads, grad_mate = gradients_call(token, rows, scales, me, parts, acts, own_slots, columns)
    layer_out, grad_tokens = total(out_pieces), total(in_pieces)
    grad_mate, grad_tokens = lax.optimization_barrier((swap_core(grad_mate), grad_tokens))
    grads = [lax.dynamic_update_slice(v, grad_mate[m], (0, (1 - core) * half, 0, 0)) for m, v in enumerate(grads)]
    return (layer_out, grad_tokens, *grads)


def scaled_sum(products, factors):
    return jnp.sum(products * factors.astype(jnp.float32)[None, :, :, None], axis=1)


def slot_term(selected, grads, factors):
    return (
        jnp.einsum("tkra,trb->krab", selected, grads, preferred_element_type=jnp.float32)
        * factors[:, :, None, None]
    )


def local_gathered(
    tokens,
    cotangent,
    gate_values,
    gate_rows,
    gate_scale,
    up_values,
    up_rows,
    up_scale,
    down_values,
    down_cols,
    down_scale,
):
    block_size = gate_values.shape[-1]
    token_count = tokens.shape[0]
    tensor_count = lax.axis_size("tensor")
    nblocks = tokens.shape[1] * tensor_count // block_size
    local_blocks = nblocks // tensor_count
    gathered = lax.all_gather(tokens, "tensor", axis=1, tiled=True)
    x_blocks = gathered.reshape(token_count, nblocks, block_size)
    gate_where, up_where, down_where = (
        lax.all_gather(gate_rows, "fsdp", axis=0, tiled=True),
        lax.all_gather(up_rows, "fsdp", axis=0, tiled=True),
        lax.all_gather(down_cols, "fsdp", axis=0, tiled=True),
    )
    gate_blocks, gate_factor, up_blocks, up_factor, down_blocks, down_factor = (
        lax.all_gather(gate_values, "fsdp", axis=0, tiled=True),
        lax.all_gather(gate_scale, "fsdp", axis=0, tiled=True),
        lax.all_gather(up_values, "fsdp", axis=0, tiled=True),
        lax.all_gather(up_scale, "fsdp", axis=0, tiled=True),
        lax.all_gather(down_values, "fsdp", axis=0, tiled=True),
        lax.all_gather(down_scale, "fsdp", axis=0, tiled=True),
    )
    gate_sel = x_blocks[:, gate_where]
    up_sel = x_blocks[:, up_where]
    gate_pre = scaled_sum(
        jnp.einsum("tkra,krab->tkrb", gate_sel, gate_blocks, preferred_element_type=jnp.float32),
        gate_factor,
    )
    up_pre = scaled_sum(
        jnp.einsum("tkra,krab->tkrb", up_sel, up_blocks, preferred_element_type=jnp.float32),
        up_factor,
    )
    sigmoid_gate = jax.nn.sigmoid(gate_pre)
    activated = gate_pre * sigmoid_gate
    hidden = (activated * up_pre).astype(jnp.bfloat16)
    down_float = down_factor.astype(jnp.float32)
    down_scaled = (
        jnp.einsum("trb,krbc->krtc", hidden, down_blocks, preferred_element_type=jnp.float32)
        * down_float[:, :, None, None]
    )
    out_full = (
        jnp.zeros((nblocks, token_count, block_size), jnp.float32).at[down_where].add(down_scaled)
    )
    out_part = lax.psum_scatter(
        out_full.astype(jnp.bfloat16), "tensor", scatter_dimension=0, tiled=True
    ).astype(jnp.float32)
    layer_out = (
        jnp.transpose(out_part, (1, 0, 2))
        .reshape(token_count, local_blocks * block_size)
        .astype(jnp.bfloat16)
    )
    grad_full = lax.all_gather(cotangent, "tensor", axis=1, tiled=True).reshape(
        token_count, nblocks, block_size
    )
    down_sel = grad_full[:, down_where]
    gate_float = gate_factor.astype(jnp.float32)
    up_float = up_factor.astype(jnp.float32)
    grad_hidden = scaled_sum(
        jnp.einsum("tkrc,krbc->tkrb", down_sel, down_blocks, preferred_element_type=jnp.float32),
        down_factor,
    )
    grad_down = lax.psum_scatter(
        (
            jnp.einsum("trb,tkrc->krbc", hidden, down_sel, preferred_element_type=jnp.float32)
            * down_float[:, :, None, None]
        ).astype(jnp.bfloat16),
        "fsdp",
        scatter_dimension=0,
        tiled=True,
    )
    grad_gate_act = (
        grad_hidden * up_pre * sigmoid_gate * (1.0 + gate_pre * (1.0 - sigmoid_gate))
    ).astype(jnp.bfloat16)
    grad_up_act = (grad_hidden * activated).astype(jnp.bfloat16)
    grad_gate = lax.psum_scatter(
        slot_term(gate_sel, grad_gate_act, gate_float).astype(jnp.bfloat16),
        "fsdp",
        scatter_dimension=0,
        tiled=True,
    )
    grad_up = lax.psum_scatter(
        slot_term(up_sel, grad_up_act, up_float).astype(jnp.bfloat16),
        "fsdp",
        scatter_dimension=0,
        tiled=True,
    )
    back_gate = (
        jnp.einsum("trb,krab->krta", grad_gate_act, gate_blocks, preferred_element_type=jnp.float32)
        * gate_float[:, :, None, None]
    )
    back_up = (
        jnp.einsum("trb,krab->krta", grad_up_act, up_blocks, preferred_element_type=jnp.float32)
        * up_float[:, :, None, None]
    )
    in_full = (
        jnp.zeros((nblocks, token_count, block_size), jnp.float32)
        .at[gate_where]
        .add(back_gate)
        .at[up_where]
        .add(back_up)
    )
    in_part = lax.psum_scatter(
        in_full.astype(jnp.bfloat16), "tensor", scatter_dimension=0, tiled=True
    ).astype(jnp.float32)
    grad_tokens = (
        jnp.transpose(in_part, (1, 0, 2))
        .reshape(token_count, local_blocks * block_size)
        .astype(jnp.bfloat16)
    )
    return (layer_out, grad_tokens, grad_gate, grad_up, grad_down)


def local(*args):
    tokens, gate_values = args[0], args[2]
    paired = lax.axis_size("fsdp") == 4 and lax.axis_size("parts") == 2
    if paired and gate_values.shape[1] % 4 == 0 and gate_values.shape[1] >= 16:
        return local_pairs(*args)
    return local_gathered(*args)


def solution(mesh):
    in_specs = (
        P(("parts", "fsdp"), "tensor"),
        P(("parts", "fsdp"), "tensor"),
        P("fsdp", "tensor", None, None),
        P("fsdp", "tensor"),
        P("fsdp", "tensor"),
        P("fsdp", "tensor", None, None),
        P("fsdp", "tensor"),
        P("fsdp", "tensor"),
        P("fsdp", "tensor", None, None),
        P("fsdp", "tensor"),
        P("fsdp", "tensor"),
    )
    out_specs = (
        P(("parts", "fsdp"), "tensor"),
        P(("parts", "fsdp"), "tensor"),
        P(("parts", "fsdp"), "tensor", None, None),
        P(("parts", "fsdp"), "tensor", None, None),
        P(("parts", "fsdp"), "tensor", None, None),
    )
    return jax.shard_map(local, mesh=mesh, in_specs=in_specs, out_specs=out_specs, check_vma=False)
```

```python
import functools

import jax
import jax.numpy as jnp
from jax import lax
from jax.experimental import pallas as pl
from jax.experimental.pallas import tpu as pltpu
from jax.sharding import PartitionSpec as P

F32, BF16 = jnp.float32, jnp.bfloat16
ANY = pl.BlockSpec(memory_space=pl.ANY)
HBM = pl.BlockSpec(memory_space=pltpu.HBM)
SMEM = pl.BlockSpec(memory_space=pltpu.SMEM)
PARAMS = pltpu.CompilerParams(vmem_limit_bytes=50 * 2**20)
STEP = 4


def dot(a, b, ca, cb):
    return lax.dot_general(a, b, (((ca,), (cb,)), ((), ())), preferred_element_type=F32)


def estimate(us):
    return pl.CostEstimate(flops=int(us * 1.1e9), bytes_accessed=int(us * 3.0e6), transcendentals=0)


def over_columns(n, step, body):
    if n // step:

        def run(j, _):
            body([j * step + u for u in range(step)])
            return 0

        lax.fori_loop(0, n // step, run, 0)
    if n % step:
        body([n - n % step + u for u in range(n % step)])


def token_copies(me, parts, which, full, sem):
    out = []
    rest = full.shape[1] // 4
    for core, part in zip((me[0], 1 - me[0]), parts):
        shards, run = part.shape[0], part.shape[1] // 2
        for shard in range(shards):
            for chip in range(2):
                here = part.at[shard, pl.ds(which * run, run), pl.ds(chip * rest, rest), :]
                to = full.at[pl.ds(shard * run, run), pl.ds(pl.multiple_of((2 * chip + core) * rest, rest), rest), :]
                out.append(pltpu.make_async_copy(here, to, sem))
    return out


def weight_copies(sizes, half_cols, base, own, mate, others, own_s, mate_s, other_s, sems):
    out = []
    start = 0
    for size, other in zip(sizes, others):

        def of(i, start=start, other=other):
            h = half_cols[i]
            sem = sems.at[i]
            copies = [pltpu.make_async_copy(w.at[:, base + h], own_s.at[i, m], sem) for m, w in enumerate(own)]
            copies.append(pltpu.make_async_copy(mate.at[:, :, h], mate_s.at[i], sem))
            copies.append(pltpu.make_async_copy(other.at[:, :, i - start], other_s.at[i], sem))
            return copies

        out.append((start, size, of))
        start += size
    return out


def start_weights(copies, more=None):
    for start, size, of in copies:

        def go(i, _, of=of):
            for c in of(i) + ([more(i)] if more else []):
                c.start()
            return 0

        lax.fori_loop(start, start + size, go, 0)


def scaled(own_s, mate_s, other_s, scale, i, m):
    count = own_s.shape[2]
    blocks = [own_s[i, m, k] for k in range(count)] + [mate_s[i, m, k] for k in range(count)]
    blocks += [other_s[i, m, k] for k in range(2 * count)]
    return [b * scale(m, k).astype(BF16) for k, b in enumerate(blocks)]


def wait_weights(own_s, mate_s, other_s, sems, i):
    for ref in (own_s, mate_s, other_s):
        pltpu.make_async_copy(ref.at[i], ref.at[i], sems.at[i]).wait()


def picker(rows, scales, h, slots):
    return (lambda m, k: rows[h * 3 * slots + m * slots + k]), (lambda m, k: scales[h * 3 * slots + m * slots + k])


def hand_out(core, acc, stage, sums_out, sems):
    if len(sums_out) == 1:
        copies = [pltpu.make_async_copy(acc, sums_out[0], sems.at[1])]
    else:
        rest = acc.shape[1] // 2
        mine, other = (pl.ds(pl.multiple_of(c * rest, rest), rest) for c in (core, 1 - core))
        stage[...] = acc[:, other, :].astype(BF16)
        copies = [pltpu.make_async_copy(stage, sums_out[1], sems.at[0]), pltpu.make_async_copy(acc.at[:, mine, :], sums_out[0], sems.at[1])]
    for c in copies:
        c.start()
    return copies


def forward_kernel(first, last, sizes, slots, parts, *refs):
    refs = list(refs)
    take = lambda n: [refs.pop(0) for _ in range(n)]
    _, half_cols, rows, scales, me = take(5)
    own = take(3)
    (mate,) = take(1)
    others = take(len(sizes))
    x_parts = take(parts)
    if not first:
        sums_in, _ = take(2)
    *sums_out, acts = take(3 if last else 2)
    x_s, acc, own_s, mate_s, other_s, act_s, stage, wsems, asems, sems = refs
    n = sum(sizes)
    copies = token_copies(me, x_parts, 0, x_s, sems.at[0])
    for c in copies:
        c.start()
    if not first:
        sums = pltpu.make_async_copy(sums_in, acc, sems.at[1])
        sums.start()
    start_weights(weight_copies(sizes, half_cols, me[1], own, mate, others, own_s, mate_s, other_s, wsems))
    if first:
        acc[...] = jnp.zeros(acc.shape, F32)
    else:
        sums.wait()
    for c in copies:
        c.wait()
    mine = x_s.shape[1] // 2
    block = x_s.shape[2]

    def body(columns):
        for i in columns:
            wait_weights(own_s, mate_s, other_s, wsems, i)
        kept = []
        for i in columns:
            row, scale = picker(rows, scales, half_cols[i], slots)
            weights = functools.partial(scaled, own_s, mate_s, other_s, scale, i)
            pre = []
            for m in range(2):
                selected = jnp.concatenate([x_s[row(m, k)] for k in range(slots)], axis=1)
                pre.append(dot(selected, jnp.concatenate(weights(m), axis=0), 1, 0))
            gate_pre, up_pre = pre
            s = jax.nn.sigmoid(gate_pre)
            activated = gate_pre * s
            hidden = (activated * up_pre).astype(BF16)
            act_s[i, 0] = hidden
            act_s[i, 1] = (up_pre * s * (1.0 + gate_pre * (1.0 - s))).astype(BF16)
            act_s[i, 2] = activated.astype(BF16)
            pltpu.make_async_copy(act_s.at[i], acts.at[half_cols[i]], asems.at[i]).start()
            kept.append((row, dot(hidden[:mine], jnp.concatenate(weights(2), axis=1), 1, 0)))
        for row, out in kept:
            for k in range(slots):
                acc[row(2, k)] += out[:, k * block : (k + 1) * block]

    over_columns(n, STEP if n % 6 else 6, body)
    finished = hand_out(me[0], acc, stage, sums_out, sems)

    def finish(i, _):
        pltpu.make_async_copy(act_s.at[i], acts.at[half_cols[i]], asems.at[i]).wait()
        return 0

    lax.fori_loop(0, n, finish, 0)
    for c in finished:
        c.wait()


def backward_kernel(first, last, sizes, slots, parts, *refs):
    refs = list(refs)
    take = lambda n: [refs.pop(0) for _ in range(n)]
    _, half_cols, rows, scales, me = take(5)
    own = take(3)
    (mate,) = take(1)
    others = take(len(sizes))
    g_parts = take(parts)
    (acts_in,) = take(1)
    if not first:
        (sums_in,) = take(1)
    *sums_out, acts = take(3 if last else 2)
    g_s, acc, own_s, mate_s, other_s, act_s, stage, wsems, asems, sems = refs
    n = sum(sizes)
    copies = token_copies(me, g_parts, 1, g_s, sems.at[0])
    for c in copies:
        c.start()

    def derivatives(i, away=False):
        here, there = act_s.at[i, pl.ds(1, 2)], acts.at[half_cols[i], pl.ds(1, 2)]
        return pltpu.make_async_copy(here, there, asems.at[i]) if away else pltpu.make_async_copy(there, here, asems.at[i])

    if not first:
        sums = pltpu.make_async_copy(sums_in, acc, sems.at[1])
        sums.start()
    weights = weight_copies(sizes, half_cols, me[1], own, mate, others, own_s, mate_s, other_s, wsems)
    start_weights(weights, derivatives)
    if first:
        acc[...] = jnp.zeros(acc.shape, F32)
    else:
        sums.wait()
    for c in copies:
        c.wait()
    mine = g_s.shape[1] // 2
    block = g_s.shape[2]

    def body(columns):
        for i in columns:
            wait_weights(own_s, mate_s, other_s, wsems, i)
            derivatives(i).wait()
        kept = []
        for i in columns:
            row, scale = picker(rows, scales, half_cols[i], slots)
            weights = functools.partial(scaled, own_s, mate_s, other_s, scale, i)
            selected = jnp.concatenate([g_s[row(2, k)] for k in range(slots)], axis=1)
            grad_hidden = dot(selected, jnp.concatenate(weights(2), axis=1), 1, 1)
            for m in range(2):
                act = (grad_hidden * act_s[i, 1 + m].astype(F32)).astype(BF16)
                act_s[i, 1 + m] = act
                kept.append((row, m, dot(act[:mine], jnp.concatenate(weights(m), axis=0), 1, 1)))
            derivatives(i, True).start()
        for row, m, back in kept:
            for k in range(slots):
                acc[row(m, k)] += back[:, k * block : (k + 1) * block]

    over_columns(n, STEP if n % 6 else 6, body)
    finished = hand_out(me[0], acc, stage, sums_out, sems)

    def finish(i, _):
        derivatives(i, True).wait()
        return 0

    lax.fori_loop(0, n, finish, 0)
    for c in finished:
        c.wait()


def columns_call(token, backward, first, last, sizes, half_cols, rows, scales, me, own, mate, others, token_parts, sums, acts):
    own_slots, _, block, _ = own[0].shape
    n = sum(sizes)
    nblocks, half_tokens = token_parts[0].shape[0] * token_parts[0].shape[1] // 2, token_parts[0].shape[2]
    tokens = 2 * half_tokens
    args = [token, half_cols, rows, scales, me, *own, mate, *others, *token_parts]
    in_specs = [SMEM] * 5 + [HBM] * 3 + [ANY] * (len(args) - 8)
    aliases = {}
    more = ([acts] if first else [acts, sums]) if backward else ([] if first else [sums, acts])
    for v in more:
        if v is acts or not last:
            aliases[len(args)] = 0 if v is sums else 1 + last
        args.append(v)
        in_specs.append(ANY)
    kernel = backward_kernel if backward else forward_kernel
    sums_out = [jax.ShapeDtypeStruct((nblocks, half_tokens, block), F32)]
    stage = (8, 16, block)
    if last:
        stage = (nblocks, half_tokens // 2, block)
        sums_out = [jax.ShapeDtypeStruct(stage, kind) for kind in (F32, BF16)]
    return pl.pallas_call(
        functools.partial(kernel, first, last, sizes, 4 * own_slots, len(token_parts)),
        in_specs=in_specs,
        out_specs=[ANY] * (len(sums_out) + 1),
        out_shape=[*sums_out, jax.ShapeDtypeStruct((mate.shape[2], 3, tokens, block), BF16)],
        scratch_shapes=[
            pltpu.VMEM((nblocks, tokens, block), BF16),
            pltpu.VMEM((nblocks, half_tokens, block), F32),
            pltpu.VMEM((n, 3, own_slots, block, block), BF16),
            pltpu.VMEM((n, 3, own_slots, block, block), BF16),
            pltpu.VMEM((n, 3, 2 * own_slots, block, block), BF16),
            pltpu.VMEM((n, 3, tokens, block), BF16),
            pltpu.VMEM(stage, BF16),
            pltpu.SemaphoreType.DMA((n,)),
            pltpu.SemaphoreType.DMA((n,)),
            pltpu.SemaphoreType.DMA((2,)),
        ],
        input_output_aliases=aliases,
        compiler_params=PARAMS,
        cost_estimate=estimate(100.0 if backward and last else 1.0),
        name="backward" if backward else "forward",
    )(*args)


def gradients_kernel(own_slots, slots, count, token, rows, scales, me, *refs):
    parts, refs = refs[:count], refs[count:]
    acts, grad_gate, grad_up, grad_down, grad_mate, x_s, g_s, act_s, out_s, asems, osems, sems = refs
    n = acts.shape[0]
    depth = act_s.shape[0]
    x_copies = token_copies(me, parts, 0, x_s, sems.at[0])
    g_copies = token_copies(me, parts, 1, g_s, sems.at[1])
    for c in x_copies + g_copies:
        c.start()
    grads = (grad_gate, grad_up, grad_down)
    block = x_s.shape[2]
    half = 2 * own_slots

    def fetch(i):
        return pltpu.make_async_copy(acts.at[i], act_s.at[lax.rem(i, depth)], asems.at[lax.rem(i, depth)])

    def stores(i):
        at = lax.rem(i, depth)
        out = [pltpu.make_async_copy(out_s.at[at, m, pl.ds(0, own_slots)], v.at[:, me[1] + i], osems.at[at]) for m, v in enumerate(grads)]
        out.append(pltpu.make_async_copy(out_s.at[at, :, pl.ds(own_slots, own_slots)], grad_mate.at[:, :, i], osems.at[at]))
        return out

    for i in range(depth):
        fetch(i).start()
    for c in x_copies + g_copies:
        c.wait()

    def body(columns):
        for i in columns:
            fetch(i).wait()

            @pl.when(i >= depth)
            def _():
                for c in stores(i - depth):
                    c.wait()

        for i in columns:
            at = lax.rem(i, depth)
            row, scale = picker(rows, scales, i, slots)
            for m, source in ((0, x_s), (1, x_s), (2, g_s)):
                act = act_s[at, (m + 1) % 3]
                selected = jnp.concatenate([source[row(m, k)] for k in range(half)], axis=1)
                out = dot(act, selected, 0, 0)
                for k in range(half):
                    piece = (out[:, k * block : (k + 1) * block] * scale(m, k)).astype(BF16)
                    out_s[at, m, k] = piece if m == 2 else piece.T
        for i in columns:
            for c in stores(i):
                c.start()

            @pl.when(i + depth < n)
            def _():
                fetch(i + depth).start()

    over_columns(n, 2, body)
    for i in range(n - depth, n):
        for c in stores(i):
            c.wait()


def gradients_call(token, rows, scales, me, parts, acts, own_slots, columns):
    n, _, tokens, block = acts.shape
    nblocks = parts[0].shape[0] * parts[0].shape[1] // 2
    depth = min(8, n)
    grad = jax.ShapeDtypeStruct((own_slots, columns, block, block), BF16)
    return pl.pallas_call(
        functools.partial(gradients_kernel, own_slots, 4 * own_slots, len(parts)),
        in_specs=[SMEM] * 4 + [ANY] * (len(parts) + 1),
        out_specs=[ANY] * 4,
        out_shape=[grad] * 3 + [jax.ShapeDtypeStruct((3, own_slots, n, block, block), BF16)],
        scratch_shapes=[
            pltpu.VMEM((nblocks, tokens, block), BF16),
            pltpu.VMEM((nblocks, tokens, block), BF16),
            pltpu.VMEM((depth, 3, tokens, block), BF16),
            pltpu.VMEM((depth, 3, 2 * own_slots, block, block), BF16),
            pltpu.SemaphoreType.DMA((depth,)),
            pltpu.SemaphoreType.DMA((depth,)),
            pltpu.SemaphoreType.DMA((2,)),
        ],
        compiler_params=PARAMS,
        cost_estimate=estimate(15.0),
        name="gradients",
    )(token, rows, scales, me, *parts, acts)


def hold(v, token):
    return lax.optimization_barrier((v, token))


def copy_kernel(pairs_of, n_in, n_out, *refs):
    me, ins, outs = refs[0], refs[1 : 1 + n_in], refs[1 + n_in : 1 + n_in + n_out]
    stages, sems = refs[1 + n_in + n_out : -1], refs[-1]
    groups = [[pltpu.make_async_copy(a, b, sems.at[j]) for a, b in pairs]
              for j, pairs in enumerate(pairs_of(me, ins, stages))]
    for group in groups:
        for c in group:
            c.start()
    away = [pltpu.make_async_copy(a, b, sems.at[n_out + j]) for j, (a, b) in enumerate(zip(stages, outs))]
    for group, c in zip(groups, away):
        for part in group:
            part.wait()
        c.start()
    for c in away:
        c.wait()


def copies_call(name, pairs_of, me, args, shapes):
    return pl.pallas_call(
        functools.partial(copy_kernel, pairs_of, len(args), len(shapes)),
        in_specs=[SMEM] + [HBM] * len(args),
        out_specs=[ANY] * len(shapes),
        out_shape=[jax.ShapeDtypeStruct(s, BF16) for s in shapes],
        scratch_shapes=[pltpu.VMEM(s, BF16) for s in shapes] + [pltpu.SemaphoreType.DMA((2 * len(shapes),))],
        compiler_params=PARAMS,
        name=name,
    )(me, *args)


def step_kernel(*refs):
    refs[-1][0] = refs[0][0]


def step(token, *arrived, us=0.1):
    return pl.pallas_call(
        step_kernel,
        in_specs=[SMEM] + [ANY] * len(arrived),
        out_specs=SMEM,
        out_shape=jax.ShapeDtypeStruct((1,), jnp.int32),
        cost_estimate=estimate(us),
        name="step",
    )(token, *arrived)


def pieces_kernel(me, keep, more, *pieces):
    run = pieces[0].shape[0]
    for s, piece in enumerate(pieces):
        at = pl.ds(lax.rem(me[4] + s, len(pieces)) * run, run)
        piece[...] = (keep[at] + more[at].astype(F32)).astype(BF16)


def pieces_call(me, keep, more, count):
    nblocks, rest, block = keep.shape
    return pl.pallas_call(
        pieces_kernel,
        in_specs=[SMEM] + [pl.BlockSpec(memory_space=pltpu.VMEM)] * 2,
        out_specs=[pl.BlockSpec(memory_space=pltpu.VMEM)] * count,
        out_shape=[jax.ShapeDtypeStruct((nblocks // count, rest, block), BF16)] * count,
        compiler_params=PARAMS,
        cost_estimate=estimate(0.1 * 3.0),
        name="pieces",
    )(me, keep, more)


def total_kernel(*refs):
    out = refs[-1]
    block = refs[0].shape[2]
    for j in range(refs[0].shape[0]):
        whole = refs[0][j].astype(F32)
        for v in refs[1:-1]:
            whole += v[j].astype(F32)
        out[:, j * block : (j + 1) * block] = whole.astype(BF16)


def total(pieces):
    run, rest, block = pieces[0].shape
    return pl.pallas_call(
        total_kernel,
        out_shape=jax.ShapeDtypeStruct((rest, run * block), BF16),
        cost_estimate=estimate(100.0),
        name="total",
    )(*pieces)


def to_blocks(v, block):
    return jnp.swapaxes(v.reshape(v.shape[0], -1, block), 0, 1)


def local_pairs(tokens, cotangent, gate_values, gate_rows, gate_scale, up_values, up_rows, up_scale,
                down_values, down_cols, down_scale):
    own = (gate_values, up_values, down_values)
    own_slots, columns, block, _ = gate_values.shape
    half = columns // 2
    per_part = half // 2
    core = lax.rem(lax.axis_index("fsdp"), 2)
    part = lax.axis_index("parts")
    first = part * per_part
    swap_core = lambda v: lax.ppermute(v, "fsdp", [(i, i ^ 1) for i in range(4)])
    swap_chip = lambda v: lax.ppermute(v, "fsdp", [(i, i ^ 2) for i in range(4)])
    swap_part = lambda v: lax.ppermute(v, "parts", [(0, 1), (1, 0)])
    me = jnp.stack([core, core * half, (1 - core) * half, first, lax.axis_index("tensor")])

    small = jnp.stack([v.astype(BF16) for v in (gate_rows, up_rows, down_cols, gate_scale, up_scale, down_scale)])
    last = jnp.zeros((block * block,), BF16).at[: small.size].set(small.reshape(-1)).reshape(1, block, block)
    both = jnp.concatenate([to_blocks(tokens, block), to_blocks(cotangent, block), last])
    received = swap_chip(both)

    def mate_pairs(me, ins, outs):
        return [[(w.at[:, pl.ds(me[2], half)], outs[0].at[m]) for m, w in enumerate(ins)]]

    sent = copies_call("mate_blocks", mate_pairs, me, own, [(3, own_slots, half, block, block)])[0]
    mate = swap_core(sent)

    packed = jnp.concatenate([small, received[-1].reshape(-1)[: small.size].reshape(small.shape)], axis=1)
    packed = jnp.stack([packed.reshape(6, 2, own_slots, columns), swap_core(packed).reshape(6, 2, own_slots, columns)], axis=2)
    packed = lax.dynamic_slice_in_dim(packed.reshape(6, -1, columns), core * half, half, axis=2).astype(F32)
    packed = jnp.transpose(packed.reshape(2, 3, -1, half), (0, 3, 1, 2)).reshape(2, -1)
    rows = packed[0].astype(jnp.int32)
    scales = packed[1]

    count = lax.axis_size("tensor")
    shift = lambda v, s: lax.ppermute(v, "tensor", [(i, (i + s) % count) for i in range(count)])

    quotas = (2 * per_part // 5,) * 2
    given = sum(quotas)
    left = per_part - given
    other_first = per_part - first
    spans = [[(first, quotas[0])], [(first + quotas[0], quotas[1])], [(first + given, left), (other_first + given, left)]]
    where = jnp.stack([start for span in spans for start, _ in span]).astype(jnp.int32)

    def chunk_pairs(me, ins, outs):
        out, j = [], 5
        for span, dst in zip(spans, outs):
            pairs, done = [], 0
            for _, size in span:
                to = pl.ds(done, size)
                pairs += [(w.at[:, pl.ds(me[1] + me[j], size)], dst.at[m, pl.ds(0, own_slots), to]) for m, w in enumerate(ins[:3])]
                pairs.append((ins[3].at[:, :, pl.ds(me[j], size)], dst.at[:, pl.ds(own_slots, own_slots), to]))
                done += size
                j += 1
            out.append(pairs)
        return out

    shapes = [(3, 2 * own_slots, sum(size for _, size in span), block, block) for span in spans]
    sends = copies_call("chunk_blocks", chunk_pairs, jnp.concatenate([me, where]), (*own, mate), shapes)
    received, sends = hold(received, sends)
    both = jnp.concatenate([both[:-1], received[:-1]], axis=1)
    pieces = [lax.all_gather(both, "tensor")]
    token = step(jnp.reshape(core, (1,)), both)
    sends, token = hold(sends, token)
    direct = [swap_chip(sends[0]), swap_chip(sends[1])]

    def call(backward, names, sums, acts, token, last=False):
        others, columns = [], []
        for name in names:
            j = int(name[1])
            others.append((direct if name[0] == "a" else relayed)[j])
            for start, size in spans[j]:
                columns.append((start if name[0] == "a" else per_part - first + start - first) + jnp.arange(size, dtype=jnp.int32))
        *sums, acts = columns_call(token, backward, sums is None, last, tuple(v.shape[2] for v in others), jnp.concatenate(columns),
                            rows, scales, me, own, mate, others, parts, sums, acts)
        return sums if last else sums[0], acts

    relayed = []

    def hand_on(j, token):
        held, token = hold(direct[j], token)
        relayed.append(swap_part(held))
        return token

    def send_on(j, token):
        held, token = hold(sends[j], token)
        direct.append(swap_chip(held))
        return token

    token = hand_on(0, step(token, direct[0], us=100.0))
    token = send_on(2, hand_on(1, step(token, direct[1])))
    token = step(token, *pieces, relayed[0], us=100.0)
    pieces, token = hold(pieces, token)
    parts = (*pieces, *(swap_core(v) for v in pieces))
    outs, acts = call(False, ("a0", "b0", "a1"), None, None, token)
    ins, acts = call(True, ("a0", "b0", "a1"), None, acts, token)
    token = step(token, ins, direct[2], relayed[1])
    (keep, send), acts = call(False, ("b1", "a2"), outs, acts, token, True)

    def scattered(keep, send):
        first, *others = pieces_call(me, keep, swap_core(send), count)
        return [first] + [shift(v, s + 1) for s, v in enumerate(others)]

    out_pieces = scattered(keep, send)
    token = step(token, out_pieces[0])
    (keep, send), acts = call(True, ("b1", "a2"), ins, acts, token, True)
    in_pieces = scattered(keep, send)
    token = step(token, in_pieces[0])
    *grads, grad_mate = gradients_call(token, rows, scales, me, parts, acts, own_slots, columns)
    layer_out, grad_tokens = total(out_pieces), total(in_pieces)
    grad_mate, grad_tokens = lax.optimization_barrier((swap_core(grad_mate), grad_tokens))
    grads = [lax.dynamic_update_slice(v, grad_mate[m], (0, (1 - core) * half, 0, 0)) for m, v in enumerate(grads)]
    return (layer_out, grad_tokens, *grads)


def scaled_sum(products, factors):
    return jnp.sum(products * factors.astype(jnp.float32)[None, :, :, None], axis=1)


def slot_term(selected, grads, factors):
    return (
        jnp.einsum("tkra,trb->krab", selected, grads, preferred_element_type=jnp.float32)
        * factors[:, :, None, None]
    )


def local_gathered(
    tokens,
    cotangent,
    gate_values,
    gate_rows,
    gate_scale,
    up_values,
    up_rows,
    up_scale,
    down_values,
    down_cols,
    down_scale,
):
    block_size = gate_values.shape[-1]
    token_count = tokens.shape[0]
    tensor_count = lax.axis_size("tensor")
    nblocks = tokens.shape[1] * tensor_count // block_size
    local_blocks = nblocks // tensor_count
    gathered = lax.all_gather(tokens, "tensor", axis=1, tiled=True)
    x_blocks = gathered.reshape(token_count, nblocks, block_size)
    gate_where, up_where, down_where = (
        lax.all_gather(gate_rows, "fsdp", axis=0, tiled=True),
        lax.all_gather(up_rows, "fsdp", axis=0, tiled=True),
        lax.all_gather(down_cols, "fsdp", axis=0, tiled=True),
    )
    gate_blocks, gate_factor, up_blocks, up_factor, down_blocks, down_factor = (
        lax.all_gather(gate_values, "fsdp", axis=0, tiled=True),
        lax.all_gather(gate_scale, "fsdp", axis=0, tiled=True),
        lax.all_gather(up_values, "fsdp", axis=0, tiled=True),
        lax.all_gather(up_scale, "fsdp", axis=0, tiled=True),
        lax.all_gather(down_values, "fsdp", axis=0, tiled=True),
        lax.all_gather(down_scale, "fsdp", axis=0, tiled=True),
    )
    gate_sel = x_blocks[:, gate_where]
    up_sel = x_blocks[:, up_where]
    gate_pre = scaled_sum(
        jnp.einsum("tkra,krab->tkrb", gate_sel, gate_blocks, preferred_element_type=jnp.float32),
        gate_factor,
    )
    up_pre = scaled_sum(
        jnp.einsum("tkra,krab->tkrb", up_sel, up_blocks, preferred_element_type=jnp.float32),
        up_factor,
    )
    sigmoid_gate = jax.nn.sigmoid(gate_pre)
    activated = gate_pre * sigmoid_gate
    hidden = (activated * up_pre).astype(jnp.bfloat16)
    down_float = down_factor.astype(jnp.float32)
    down_scaled = (
        jnp.einsum("trb,krbc->krtc", hidden, down_blocks, preferred_element_type=jnp.float32)
        * down_float[:, :, None, None]
    )
    out_full = (
        jnp.zeros((nblocks, token_count, block_size), jnp.float32).at[down_where].add(down_scaled)
    )
    out_part = lax.psum_scatter(
        out_full.astype(jnp.bfloat16), "tensor", scatter_dimension=0, tiled=True
    ).astype(jnp.float32)
    layer_out = (
        jnp.transpose(out_part, (1, 0, 2))
        .reshape(token_count, local_blocks * block_size)
        .astype(jnp.bfloat16)
    )
    grad_full = lax.all_gather(cotangent, "tensor", axis=1, tiled=True).reshape(
        token_count, nblocks, block_size
    )
    down_sel = grad_full[:, down_where]
    gate_float = gate_factor.astype(jnp.float32)
    up_float = up_factor.astype(jnp.float32)
    grad_hidden = scaled_sum(
        jnp.einsum("tkrc,krbc->tkrb", down_sel, down_blocks, preferred_element_type=jnp.float32),
        down_factor,
    )
    grad_down = lax.psum_scatter(
        (
            jnp.einsum("trb,tkrc->krbc", hidden, down_sel, preferred_element_type=jnp.float32)
            * down_float[:, :, None, None]
        ).astype(jnp.bfloat16),
        "fsdp",
        scatter_dimension=0,
        tiled=True,
    )
    grad_gate_act = (
        grad_hidden * up_pre * sigmoid_gate * (1.0 + gate_pre * (1.0 - sigmoid_gate))
    ).astype(jnp.bfloat16)
    grad_up_act = (grad_hidden * activated).astype(jnp.bfloat16)
    grad_gate = lax.psum_scatter(
        slot_term(gate_sel, grad_gate_act, gate_float).astype(jnp.bfloat16),
        "fsdp",
        scatter_dimension=0,
        tiled=True,
    )
    grad_up = lax.psum_scatter(
        slot_term(up_sel, grad_up_act, up_float).astype(jnp.bfloat16),
        "fsdp",
        scatter_dimension=0,
        tiled=True,
    )
    back_gate = (
        jnp.einsum("trb,krab->krta", grad_gate_act, gate_blocks, preferred_element_type=jnp.float32)
        * gate_float[:, :, None, None]
    )
    back_up = (
        jnp.einsum("trb,krab->krta", grad_up_act, up_blocks, preferred_element_type=jnp.float32)
        * up_float[:, :, None, None]
    )
    in_full = (
        jnp.zeros((nblocks, token_count, block_size), jnp.float32)
        .at[gate_where]
        .add(back_gate)
        .at[up_where]
        .add(back_up)
    )
    in_part = lax.psum_scatter(
        in_full.astype(jnp.bfloat16), "tensor", scatter_dimension=0, tiled=True
    ).astype(jnp.float32)
    grad_tokens = (
        jnp.transpose(in_part, (1, 0, 2))
        .reshape(token_count, local_blocks * block_size)
        .astype(jnp.bfloat16)
    )
    return (layer_out, grad_tokens, grad_gate, grad_up, grad_down)


def local(*args):
    tokens, gate_values = args[0], args[2]
    paired = lax.axis_size("fsdp") == 4 and lax.axis_size("parts") == 2
    if paired and gate_values.shape[1] % 4 == 0 and gate_values.shape[1] >= 16:
        return local_pairs(*args)
    return local_gathered(*args)


def solution(mesh):
    in_specs = (
        P(("parts", "fsdp"), "tensor"),
        P(("parts", "fsdp"), "tensor"),
        P("fsdp", "tensor", None, None),
        P("fsdp", "tensor"),
        P("fsdp", "tensor"),
        P("fsdp", "tensor", None, None),
        P("fsdp", "tensor"),
        P("fsdp", "tensor"),
        P("fsdp", "tensor", None, None),
        P("fsdp", "tensor"),
        P("fsdp", "tensor"),
    )
    out_specs = (
        P(("parts", "fsdp"), "tensor"),
        P(("parts", "fsdp"), "tensor"),
        P(("parts", "fsdp"), "tensor", None, None),
        P(("parts", "fsdp"), "tensor", None, None),
        P(("parts", "fsdp"), "tensor", None, None),
    )
    return jax.shard_map(local, mesh=mesh, in_specs=in_specs, out_specs=out_specs, check_vma=False)
```
